512 devices in a mesh: dp: 32 (over y_hi, z, core), tensor: 16 (over x, y_lo).
Axes of the slice: x: 4, y: 8 (y_hi: 2, y_lo: 4; y = y_hi * 4 + y_lo), z: 8, core: 2. Of those that a mesh axis runs over, the one named last changes fastest.
Arguments:
- hidden_acts: bfloat16 [65536, 14336], P('dp', 'tensor'), may hold values from -6 to 6
- out_grads: bfloat16 [65536, 4096], P('dp', 'tensor'), may hold values from -6 to 6
- proj_in: bfloat16 [14336, 64], P('tensor'), may hold values from -0.046875 to 0.046875
- proj_out: bfloat16 [4096, 64], P('tensor'), may hold values from -0.09375 to 0.09375
- segments: int32 [32, 65536], P(None, 'dp'), may hold values from 0 to 1, as said below
- doc_counts: int32 [32], P('dp'), may hold values from 10 to 32
Outputs:
- doc_grads: bfloat16 [1024, 4096], P('dp', 'tensor')
- fisher: float32 [4096, 4096], P('dp', 'tensor')
The draws below stay inside these ranges and needn't reach their ends.
Inputs may be any that keep to these rules, and one draw needn't show every extreme that they name: `segments`: every token belongs to exactly one slot of its shard; within one shard's 2048 tokens the slots 0 to 31 are contiguous runs in that order, each holding at least one token.
All inputs are finite; a program needn't handle non-finite values.
Results may differ from the reference program's by a relative error of at most 0.0062.
Values may be sent and summed in bfloat16 or wider, within the bound.
A program may use at most 64 MiB of HBM per device.

```python
import jax
import jax.numpy as jnp
from jax import lax

D = 4096
FF = 14336
RANK = 64
TOK_DEV = 2048
DOCS_DEV = 32
TOKENS = 65536


def doc_layout(key):
    shards = TOKENS // TOK_DEV

    def one_shard(subkey):
        shuffled = jax.random.permutation(subkey, TOK_DEV - 1)
        cut_points = shuffled[:DOCS_DEV - 1] + 1
        boundary = jnp.zeros((TOK_DEV,), jnp.int32).at[cut_points].set(1)
        slot_of = jnp.cumsum(boundary).astype(jnp.int32)
        return (jnp.arange(DOCS_DEV, dtype=jnp.int32)[:, None] == slot_of[None, :]).astype(jnp.int32)
    blocks = jax.vmap(one_shard)(jax.random.split(key, shards))
    return blocks.transpose(1, 0, 2).reshape(DOCS_DEV, TOKENS)


def draw_segments(key, part):
    return doc_layout(jax.random.fold_in(key, 11))


def draw_doc_counts(key, part):
    shards = TOKENS // TOK_DEV
    least_docs = max(1, DOCS_DEV // 3)
    position = jnp.arange(shards, dtype=jnp.int32)
    rising = least_docs + position * (DOCS_DEV - least_docs) // max(shards - 1, 1)
    reach = max(1, DOCS_DEV // 12)
    jitter = jax.random.randint(jax.random.fold_in(key, 23), (shards,), -reach, reach + 1, dtype=jnp.int32)
    counts_drawn = jnp.clip(rising + jitter, least_docs, DOCS_DEV)
    counts_drawn = counts_drawn.at[0].set(least_docs).at[shards - 1].set(DOCS_DEV)
    return counts_drawn.astype(jnp.int32)


def shard_levels(own_key, shape, cuts, smallest, high):
    def one(dim, shards_of):
        draws = jax.random.uniform(jax.random.fold_in(jax.random.fold_in(own_key, 6), dim), (shards_of,), jnp.float32, smallest / len(cuts), high / len(cuts))
        return jnp.repeat(jnp.exp(draws), shape[dim] // shards_of).reshape((-1,) + (1,) * (len(shape) - dim - 1))

    factor_of = one(*cuts[0])
    for cut in cuts[1:]:
        factor_of = factor_of * one(*cut)
    return factor_of


def noise(key, dims, deviation, bound, cuts=(), kind=jnp.bfloat16):
    gain = shard_levels(key, dims, cuts, -0.22, 0.18) if cuts else 1.0
    drawn = jax.random.normal(key, dims, jnp.float32) * deviation * gain
    return jnp.minimum(jnp.maximum(drawn, -bound), bound).astype(kind)


def setup_inputs(seed: int = 0) -> dict:
    arg_keys = jax.random.split(jax.random.key(seed), 7)
    return {
        "hidden_acts": noise(arg_keys[0], (TOKENS, FF), 1.0, 6.0, ((0, 32), (1, 16))),
        "out_grads": noise(arg_keys[1], (TOKENS, D), 1.0, 6.0, ((0, 32), (1, 16))),
        "proj_in": noise(arg_keys[2], (FF, RANK), FF ** -0.5, 0.046875, ((0, 16),)),
        "proj_out": noise(arg_keys[3], (D, RANK), D ** -0.5, 0.09375, ((0, 16),)),
        "segments": draw_segments(jax.random.fold_in(arg_keys[6], 71), 0),
        "doc_counts": draw_doc_counts(jax.random.fold_in(arg_keys[6], 71), 0),
    }


def reference(hidden_acts, out_grads, proj_in, proj_out, segments, doc_counts):
    shard_total = doc_counts.shape[0]
    shard_tokens = hidden_acts.shape[0] // shard_total
    x_proj = jnp.dot(hidden_acts, proj_in, preferred_element_type=jnp.float32)
    dy_proj = jnp.dot(out_grads, proj_out, preferred_element_type=jnp.float32)
    doc_index = jnp.arange(segments.shape[0], dtype=jnp.int32)

    def per_shard(shard_idx):
        offset = (shard_idx * shard_tokens).astype(jnp.int32)
        x_rows = lax.dynamic_slice_in_dim(x_proj, offset, shard_tokens, 0)
        dy_rows = lax.dynamic_slice_in_dim(dy_proj, offset, shard_tokens, 0)
        seg_rows = lax.dynamic_slice_in_dim(segments, offset, shard_tokens, 1)
        live_docs = (doc_index < doc_counts[shard_idx]).astype(jnp.int32)
        seg_live = seg_rows * live_docs[:, None]
        outer = (dy_rows[:, :, None] * x_rows[:, None, :]).reshape(shard_tokens, -1).astype(jnp.bfloat16)
        doc_terms = jnp.dot(seg_live.astype(jnp.bfloat16), outer, preferred_element_type=jnp.float32)
        return doc_terms, jnp.sum(seg_live).astype(jnp.float32)

    doc_sums, live_tokens = lax.map(per_shard, jnp.arange(shard_total, dtype=jnp.int32))
    doc_grads = doc_sums.reshape(-1, doc_sums.shape[-1]).astype(jnp.bfloat16)
    total_tokens = jnp.sum(live_tokens)
    fisher = jnp.dot(doc_grads.T, doc_grads, preferred_element_type=jnp.float32) / total_tokens
    return doc_grads, fisher
```

```python
import jax
import jax.numpy as jnp
from jax import lax
from jax.experimental import pallas as pl
from jax.experimental.pallas import tpu as pltpu
from jax.sharding import PartitionSpec as P

MESH = pl.DeviceIdType.MESH
F32 = jnp.float32
BF16 = jnp.bfloat16
RANK = 64
QUART = 16
CHUNKS = 4
DOCS = 32
COLS = 256
NT = (((1,), (1,)), ((), ()))
TN = (((0,), (0,)), ((), ()))


def dot(left, right, dims):
    return lax.dot_general(left, right, dims, preferred_element_type=F32)


def to_doc_rows(tile):
    turned = tile.astype(F32).T
    return jnp.concatenate([turned[DOCS * a : DOCS * (a + 1)] for a in range(4)], axis=1).astype(BF16)


def kernel(
    acts, grads, pin, pout, seg, counts, doc_out, fis_out,
    acts_v, grads_v, dy_part, x_part, x_send, dy_got, x_got, dy_send2, x_send2, dy_got2, x_got2,
    live_v, wide, sums, c_own, c_turn, g_col, g_row, f_part, f_got,
    in_sem, send_sem, recv_sem,
):
    i, j = lax.axis_index("dp"), lax.axis_index("tensor")
    k, c = i // 2, i % 2
    jx, jy = j // 4, j % 4
    x_peers = [(i, (jx + d) % 4 * 4 + jy) for d in (1, 2, 3)]
    y_peers = [(i, jx * 4 + (jy + d) % 4) for d in (1, 2, 3)]
    xy_peers = [(i, (j + d) % 16) for d in range(1, 16)]
    dp_peers = [((k + d) % 16 * 2 + c, j) for d in range(1, 16)]
    sibling = (2 * k + 1 - c, j)
    turn_to = [((jx * 4 + (jy + d) % 4) * 2 + c, k) for d in range(4)]
    turn_from = [(j * 2 + c, k // 4 * 4 + (k + d) % 4) for d in range(4)]
    on_diagonal = j == k

    rows = acts.shape[0] // CHUNKS
    loads = [pltpu.make_async_copy(grads, grads_v, in_sem.at[CHUNKS])]
    loads += [
        pltpu.make_async_copy(acts.at[pl.ds(n * rows, rows)], acts_v.at[pl.ds(n * rows, rows)], in_sem.at[n])
        for n in range(CHUNKS)
    ]
    for load in loads:
        load.start()

    barrier = pltpu.get_barrier_semaphore()

    def greet(peer):
        pl.semaphore_signal(barrier, inc=1, device_id=peer, device_id_type=MESH)

    for peer in xy_peers + dp_peers + [sibling] + turn_to[1:] + turn_from[1:]:
        greet(peer)

    @pl.when(jnp.logical_not(on_diagonal))
    def _():
        greet(turn_to[0])
        greet(turn_from[0])

    def remote(src, dst, sem, peer):
        return pltpu.make_async_remote_copy(
            src_ref=src, dst_ref=dst, send_sem=send_sem.at[sem], recv_sem=recv_sem.at[sem],
            device_id=peer, device_id_type=MESH,
        )

    def wait_for(buffer, sems, sem):
        pltpu.make_async_copy(buffer, buffer, sems.at[sem]).wait()

    pout_t = pout[...].astype(F32).T.astype(BF16)
    pin_t = pin[...].astype(F32).T.astype(BF16)
    loads[0].wait()
    for n in range(CHUNKS):
        part = pl.ds(n * rows, rows)
        dy_part[:, part] = dot(pout_t, grads_v[part, :], NT)

    pl.semaphore_wait(barrier, jnp.where(on_diagonal, 37, 39))

    def block(index):
        return pl.ds(pl.multiple_of(index * QUART, QUART), QUART)

    for d, peer in enumerate(x_peers):
        remote(dy_part.at[block((jx + d + 1) % 4)], dy_got.at[d], 0, peer).start()

    for n in range(CHUNKS):
        part = pl.ds(n * rows, rows)
        loads[n + 1].wait()
        product = dot(pin_t, acts_v[part, :], NT)
        x_part[:, part] = product
        x_send[:, part] = product.astype(BF16)
    for d, peer in enumerate(y_peers):
        remote(x_send.at[block((jy + d + 1) % 4)], x_got.at[d], 1, peer).start()

    live = jnp.where(lax.broadcasted_iota(jnp.int32, seg.shape, 0) < counts[0], seg[...], 0).astype(F32)
    live_v[...] = live
    tokens = jnp.sum(live)

    wait_for(dy_got, recv_sem, 0)
    dy_sum = dy_part[block(jx), :] + dy_got[0] + dy_got[1] + dy_got[2]
    dy_send2[...] = dy_sum.astype(BF16)
    for d, peer in enumerate(y_peers):
        remote(dy_send2, dy_got2.at[d], 2, peer).start()

    wait_for(x_got, recv_sem, 1)
    x_send2[...] = x_part[block(jy), :] + x_got[0].astype(F32) + x_got[1].astype(F32) + x_got[2].astype(F32)
    for d, peer in enumerate(x_peers):
        remote(x_send2, x_got2.at[d], 3, peer).start()

    wait_for(dy_got2, recv_sem, 2)
    dy_all = dy_sum + dy_got2[0].astype(F32) + dy_got2[1].astype(F32) + dy_got2[2].astype(F32)
    for a in range(QUART):
        wide[a * DOCS : (a + 1) * DOCS, :] = (live_v[...] * dy_all[a : a + 1, :]).astype(BF16)
    wait_for(x_got2, recv_sem, 3)
    x_all = x_send2[...] + x_got2[0] + x_got2[1] + x_got2[2]
    x_high = x_all.astype(BF16)
    x_low = (x_all - x_high.astype(F32)).astype(BF16)
    both = dot(jnp.concatenate([x_high, x_low], axis=0), wide[...], NT)
    total = (both[:QUART] + both[QUART:]).astype(BF16)
    for q in range(4):
        sums[q] = total[:, q * 128 : (q + 1) * 128]

    for d in (1, 2, 3):
        remote(sums.at[(jy + d) % 4], c_turn.at[jy], 5, turn_to[d]).start()

    @pl.when(jnp.logical_not(on_diagonal))
    def _():
        remote(sums.at[jy], c_turn.at[jy], 9, turn_to[0]).start()

    for d, peer in enumerate(y_peers):
        remote(sums.at[(jy + d + 1) % 4], c_own.at[jy], 4, peer).start()
    c_own[jy] = sums[jy]

    @pl.when(on_diagonal)
    def _():
        c_turn[jy] = sums[jy]

    wait_for(c_own.at[pl.ds(0, 3)], recv_sem, 4)
    own = to_doc_rows(c_own[...].reshape(RANK, 128))
    doc_out[...] = own
    high = jnp.floor(tokens * (1.0 / 256.0)) * 256.0
    corner = lax.broadcasted_iota(jnp.int32, (QUART, COLS), 0) * COLS + lax.broadcasted_iota(
        jnp.int32, (QUART, COLS), 1
    )
    tail = jnp.where(corner == 0, high, jnp.where(corner == 1, tokens - high, 0.0)).astype(BF16)
    g_col[k] = jnp.concatenate([own, tail], axis=0)
    for peer in dp_peers:
        remote(g_col.at[k], g_col.at[k], 6, peer).start()

    wait_for(c_turn.at[pl.ds(0, 3)], recv_sem, 5)

    @pl.when(jnp.logical_not(on_diagonal))
    def _():
        wait_for(c_turn.at[0], recv_sem, 9)

    g_row[j] = to_doc_rows(c_turn[...].reshape(RANK, 128))
    for peer in xy_peers:
        remote(g_row.at[j], g_row.at[j], 7, peer).start()

    wait_for(g_col.at[pl.ds(0, 15)], recv_sem, 6)
    columns = g_col[:, :DOCS, :].reshape(16 * DOCS, COLS)
    live_tokens = jnp.sum(g_col[:, DOCS:, :].astype(F32))
    wait_for(g_row.at[pl.ds(0, 15)], recv_sem, 7)
    product = dot(g_row[...].reshape(16 * DOCS, COLS), columns, TN)
    f_part[0, :128] = product[:128]
    f_part[1, :128] = product[128:]
    f_part[:, 128:] = jnp.full((2, 8, COLS), live_tokens, F32)
    swap = remote(f_part.at[1 - c], f_got, 8, sibling)
    swap.start()
    wait_for(f_got, recv_sem, 8)
    count = f_got[128:129, :] + live_tokens
    fis_out[...] = (f_part[c, :128] + f_got[:128]) / count

    for buffer, sem in (
        (dy_got, 0), (x_got, 1), (dy_got2, 2), (x_got2, 3), (c_own.at[pl.ds(0, 3)], 4),
        (c_turn.at[pl.ds(0, 3)], 5), (g_col.at[pl.ds(0, 15)], 6), (g_row.at[pl.ds(0, 15)], 7), (f_got, 8),
    ):
        wait_for(buffer, send_sem, sem)

    @pl.when(jnp.logical_not(on_diagonal))
    def _():
        wait_for(c_turn.at[0], send_sem, 9)


def per_device(acts, grads, pin, pout, seg, counts):
    tok, hidden = acts.shape
    width = grads.shape[1]
    vmem, any_, smem = (pl.BlockSpec(memory_space=m) for m in (pltpu.VMEM, pl.ANY, pltpu.SMEM))
    return pl.pallas_call(
        kernel,
        out_shape=(
            jax.ShapeDtypeStruct((DOCS, COLS), BF16),
            jax.ShapeDtypeStruct((128, COLS), F32),
        ),
        in_specs=[any_, any_, vmem, vmem, vmem, smem],
        out_specs=(vmem, vmem),
        scratch_shapes=[
            pltpu.VMEM((tok, hidden), BF16),
            pltpu.VMEM((tok, width), BF16),
            pltpu.VMEM((RANK, tok), F32),
            pltpu.VMEM((RANK, tok), F32),
            pltpu.VMEM((RANK, tok), BF16),
            pltpu.VMEM((3, QUART, tok), F32),
            pltpu.VMEM((3, QUART, tok), BF16),
            pltpu.VMEM((QUART, tok), BF16),
            pltpu.VMEM((QUART, tok), F32),
            pltpu.VMEM((3, QUART, tok), BF16),
            pltpu.VMEM((3, QUART, tok), F32),
            pltpu.VMEM((DOCS, tok), F32),
            pltpu.VMEM((QUART * DOCS, tok), BF16),
            pltpu.VMEM((4, QUART, 128), BF16),
            pltpu.VMEM((4, QUART, 128), BF16),
            pltpu.VMEM((4, QUART, 128), BF16),
            pltpu.VMEM((16, DOCS + QUART, COLS), BF16),
            pltpu.VMEM((16, DOCS, COLS), BF16),
            pltpu.VMEM((2, 136, COLS), F32),
            pltpu.VMEM((136, COLS), F32),
            pltpu.SemaphoreType.DMA((CHUNKS + 1,)),
            pltpu.SemaphoreType.DMA((10,)),
            pltpu.SemaphoreType.DMA((10,)),
        ],
        compiler_params=pltpu.CompilerParams(
            collective_id=0, has_side_effects=True, vmem_limit_bytes=40 * 1024 * 1024
        ),
        cost_estimate=pl.CostEstimate(flops=10**9, bytes_accessed=6 * 10**6, transcendentals=0),
        name="logra",
    )(acts, grads, pin, pout, seg, counts)


def solution(mesh):
    return jax.shard_map(
        per_device,
        mesh=mesh,
        in_specs=(
            P("dp", "tensor"),
            P("dp", "tensor"),
            P("tensor", None),
            P("tensor", None),
            P(None, "dp"),
            P("dp"),
        ),
        out_specs=(P("dp", "tensor"), P("dp", "tensor")),
        check_vma=False,
    )
```

```python
import jax
import jax.numpy as jnp
from jax import lax
from jax.experimental import pallas as pl
from jax.experimental.pallas import tpu as pltpu
from jax.sharding import PartitionSpec as P

MESH = pl.DeviceIdType.MESH
F32 = jnp.float32
BF16 = jnp.bfloat16
RANK = 64
QUART = 16
CHUNKS = 4
DOCS = 32
COLS = 256
NT = (((1,), (1,)), ((), ()))
TN = (((0,), (0,)), ((), ()))


def dot(left, right, dims):
    return lax.dot_general(left, right, dims, preferred_element_type=F32)


def to_doc_rows(tile):
    turned = tile.astype(F32).T
    return jnp.concatenate([turned[DOCS * a : DOCS * (a + 1)] for a in range(4)], axis=1).astype(BF16)


def kernel(
    acts, grads, pin, pout, seg, counts, doc_out, fis_out,
    acts_v, grads_v, pin_v, pout_v, seg_v, dy_part, x_part, x_send, dy_got, x_got, dy_send2, x_send2, dy_got2, x_got2,
    live_v, wide, sums, c_own, c_turn, g_col, g_row, f_part, f_got,
    in_sem, send_sem, recv_sem,
):
    i, j = lax.axis_index("dp"), lax.axis_index("tensor")
    k, c = i // 2, i % 2
    jx, jy = j // 4, j % 4
    x_peers = [(i, (jx + d) % 4 * 4 + jy) for d in (1, 2, 3)]
    y_peers = [(i, jx * 4 + (jy + d) % 4) for d in (1, 2, 3)]
    xy_peers = [(i, (j + d) % 16) for d in range(1, 16)]
    dp_peers = [((k + d) % 16 * 2 + c, j) for d in range(1, 16)]
    sibling = (2 * k + 1 - c, j)
    turn_to = [((jx * 4 + (jy + d) % 4) * 2 + c, k) for d in range(4)]
    turn_from = [(j * 2 + c, k // 4 * 4 + (k + d) % 4) for d in range(4)]
    on_diagonal = j == k

    rows = acts.shape[0] // CHUNKS
    loads = [
        pltpu.make_async_copy(src, dst, in_sem.at[CHUNKS + n])
        for n, (src, dst) in enumerate(((pout, pout_v), (grads, grads_v), (pin, pin_v), (seg, seg_v)))
    ]
    loads += [
        pltpu.make_async_copy(acts.at[pl.ds(n * rows, rows)], acts_v.at[pl.ds(n * rows, rows)], in_sem.at[n])
        for n in range(CHUNKS)
    ]
    for load in loads:
        load.start()

    barrier = pltpu.get_barrier_semaphore()

    def greet(peer):
        pl.semaphore_signal(barrier, inc=1, device_id=peer, device_id_type=MESH)

    for peer in xy_peers + dp_peers + [sibling] + turn_to[1:] + turn_from[1:]:
        greet(peer)

    @pl.when(jnp.logical_not(on_diagonal))
    def _():
        greet(turn_to[0])
        greet(turn_from[0])

    def remote(src, dst, sem, peer):
        return pltpu.make_async_remote_copy(
            src_ref=src, dst_ref=dst, send_sem=send_sem.at[sem], recv_sem=recv_sem.at[sem],
            device_id=peer, device_id_type=MESH,
        )

    def wait_for(buffer, sems, sem):
        pltpu.make_async_copy(buffer, buffer, sems.at[sem]).wait()

    loads[0].wait()
    loads[1].wait()
    for n in range(CHUNKS):
        part = pl.ds(n * rows, rows)
        dy_part[:, part] = dot(pout_v[...], grads_v[part, :], NT)

    pl.semaphore_wait(barrier, jnp.where(on_diagonal, 37, 39))

    def block(index):
        return pl.ds(pl.multiple_of(index * QUART, QUART), QUART)

    for d, peer in enumerate(x_peers):
        remote(dy_part.at[block((jx + d + 1) % 4)], dy_got.at[d], 0, peer).start()

    loads[2].wait()
    for n in range(CHUNKS):
        part = pl.ds(n * rows, rows)
        loads[n + 4].wait()
        product = dot(pin_v[...], acts_v[part, :], NT)
        x_part[:, part] = product
        x_send[:, part] = product.astype(BF16)
    for d, peer in enumerate(y_peers):
        remote(x_send.at[block((jy + d + 1) % 4)], x_got.at[d], 1, peer).start()

    loads[3].wait()
    live = jnp.where(lax.broadcasted_iota(jnp.int32, seg.shape, 0) < counts[0], seg_v[...], 0).astype(F32)
    live_v[...] = live
    tokens = jnp.sum(live)

    wait_for(dy_got, recv_sem, 0)
    dy_sum = dy_part[block(jx), :] + dy_got[0] + dy_got[1] + dy_got[2]
    dy_send2[...] = dy_sum.astype(BF16)
    for d, peer in enumerate(y_peers):
        remote(dy_send2, dy_got2.at[d], 2, peer).start()

    wait_for(x_got, recv_sem, 1)
    x_send2[...] = x_part[block(jy), :] + x_got[0].astype(F32) + x_got[1].astype(F32) + x_got[2].astype(F32)
    for d, peer in enumerate(x_peers):
        remote(x_send2, x_got2.at[d], 3, peer).start()

    wait_for(dy_got2, recv_sem, 2)
    dy_all = dy_sum + dy_got2[0].astype(F32) + dy_got2[1].astype(F32) + dy_got2[2].astype(F32)
    for a in range(QUART):
        wide[a * DOCS : (a + 1) * DOCS, :] = (live_v[...] * dy_all[a : a + 1, :]).astype(BF16)
    wait_for(x_got2, recv_sem, 3)
    x_all = x_send2[...] + x_got2[0] + x_got2[1] + x_got2[2]
    x_high = x_all.astype(BF16)
    x_low = (x_all - x_high.astype(F32)).astype(BF16)
    both = dot(jnp.concatenate([x_high, x_low], axis=0), wide[...], NT)
    total = (both[:QUART] + both[QUART:]).astype(BF16)
    for q in range(4):
        sums[q] = total[:, q * 128 : (q + 1) * 128]

    for d in (1, 2, 3):
        remote(sums.at[(jy + d) % 4], c_turn.at[jy], 5, turn_to[d]).start()

    @pl.when(jnp.logical_not(on_diagonal))
    def _():
        remote(sums.at[jy], c_turn.at[jy], 9, turn_to[0]).start()

    for d, peer in enumerate(y_peers):
        remote(sums.at[(jy + d + 1) % 4], c_own.at[jy], 4, peer).start()
    c_own[jy] = sums[jy]

    @pl.when(on_diagonal)
    def _():
        c_turn[jy] = sums[jy]

    wait_for(c_own.at[pl.ds(0, 3)], recv_sem, 4)
    own = to_doc_rows(c_own[...].reshape(RANK, 128))
    doc_out[...] = own
    high = jnp.floor(tokens * (1.0 / 256.0)) * 256.0
    corner = lax.broadcasted_iota(jnp.int32, (QUART, COLS), 0) * COLS + lax.broadcasted_iota(
        jnp.int32, (QUART, COLS), 1
    )
    tail = jnp.where(corner == 0, high, jnp.where(corner == 1, tokens - high, 0.0)).astype(BF16)
    g_col[k] = jnp.concatenate([own, tail], axis=0)
    for peer in dp_peers:
        remote(g_col.at[k], g_col.at[k], 6, peer).start()

    wait_for(c_turn.at[pl.ds(0, 3)], recv_sem, 5)

    @pl.when(jnp.logical_not(on_diagonal))
    def _():
        wait_for(c_turn.at[0], recv_sem, 9)

    g_row[j] = to_doc_rows(c_turn[...].reshape(RANK, 128))
    for peer in xy_peers:
        remote(g_row.at[j], g_row.at[j], 7, peer).start()

    wait_for(g_col.at[pl.ds(0, 15)], recv_sem, 6)
    columns = g_col[:, :DOCS, :].reshape(16 * DOCS, COLS)
    live_tokens = jnp.sum(g_col[:, DOCS:, :].astype(F32))
    wait_for(g_row.at[pl.ds(0, 15)], recv_sem, 7)
    product = dot(g_row[...].reshape(16 * DOCS, COLS), columns, TN)
    f_part[0, :128] = product[:128]
    f_part[1, :128] = product[128:]
    f_part[:, 128:] = jnp.full((2, 8, COLS), live_tokens, F32)
    remote(f_part.at[1 - c], f_got, 8, sibling).start()
    wait_for(f_got, recv_sem, 8)
    fis_out[...] = (f_part[c, :128] + f_got[:128]) / (f_got[128:129, :] + live_tokens)

    for buffer, sem in (
        (dy_got, 0), (x_got, 1), (dy_got2, 2), (x_got2, 3), (c_own.at[pl.ds(0, 3)], 4),
        (c_turn.at[pl.ds(0, 3)], 5), (g_col.at[pl.ds(0, 15)], 6), (g_row.at[pl.ds(0, 15)], 7), (f_got, 8),
    ):
        wait_for(buffer, send_sem, sem)

    @pl.when(jnp.logical_not(on_diagonal))
    def _():
        wait_for(c_turn.at[0], send_sem, 9)


def per_device(acts, grads, pin, pout, seg, counts):
    tok, hidden = acts.shape
    width = grads.shape[1]
    vmem, hbm, smem = (pl.BlockSpec(memory_space=m) for m in (pltpu.VMEM, pltpu.HBM, pltpu.SMEM))
    return pl.pallas_call(
        kernel,
        out_shape=(
            jax.ShapeDtypeStruct((DOCS, COLS), BF16),
            jax.ShapeDtypeStruct((128, COLS), F32),
        ),
        in_specs=[hbm, hbm, hbm, hbm, hbm, smem],
        out_specs=(vmem, vmem),
        scratch_shapes=[
            pltpu.VMEM((tok, hidden), BF16),
            pltpu.VMEM((tok, width), BF16),
            pltpu.VMEM((RANK, hidden), BF16),
            pltpu.VMEM((RANK, width), BF16),
            pltpu.VMEM((DOCS, tok), jnp.int32),
            pltpu.VMEM((RANK, tok), F32),
            pltpu.VMEM((RANK, tok), F32),
            pltpu.VMEM((RANK, tok), BF16),
            pltpu.VMEM((3, QUART, tok), F32),
            pltpu.VMEM((3, QUART, tok), BF16),
            pltpu.VMEM((QUART, tok), BF16),
            pltpu.VMEM((QUART, tok), F32),
            pltpu.VMEM((3, QUART, tok), BF16),
            pltpu.VMEM((3, QUART, tok), F32),
            pltpu.VMEM((DOCS, tok), F32),
            pltpu.VMEM((QUART * DOCS, tok), BF16),
            pltpu.VMEM((4, QUART, 128), BF16),
            pltpu.VMEM((4, QUART, 128), BF16),
            pltpu.VMEM((4, QUART, 128), BF16),
            pltpu.VMEM((16, DOCS + QUART, COLS), BF16),
            pltpu.VMEM((16, DOCS, COLS), BF16),
            pltpu.VMEM((2, 136, COLS), F32),
            pltpu.VMEM((136, COLS), F32),
            pltpu.SemaphoreType.DMA((CHUNKS + 4,)),
            pltpu.SemaphoreType.DMA((10,)),
            pltpu.SemaphoreType.DMA((10,)),
        ],
        compiler_params=pltpu.CompilerParams(
            collective_id=0, has_side_effects=True, vmem_limit_bytes=61 * 1024 * 1024
        ),
        cost_estimate=pl.CostEstimate(flops=10**9, bytes_accessed=6 * 10**6, transcendentals=0),
        name="logra",
    )(acts, grads, pin.T, pout.T, seg, counts)


def solution(mesh):
    return jax.shard_map(
        per_device,
        mesh=mesh,
        in_specs=(
            P("dp", "tensor"),
            P("dp", "tensor"),
            P("tensor", None),
            P("tensor", None),
            P(None, "dp"),
            P("dp"),
        ),
        out_specs=(P("dp", "tensor"), P("dp", "tensor")),
        check_vma=False,
    )
```

```python
import jax
import jax.numpy as jnp
from jax import lax
from jax.experimental import pallas as pl
from jax.experimental.pallas import tpu as pltpu
from jax.sharding import PartitionSpec as P

MESH = pl.DeviceIdType.MESH
F32 = jnp.float32
BF16 = jnp.bfloat16
RANK = 64
QUART = 16
CHUNKS = 4
HALVES = 2
DOCS = 32
COLS = 256
NT = (((1,), (1,)), ((), ()))
TN = (((0,), (0,)), ((), ()))


def dot(left, right, dims):
    return lax.dot_general(left, right, dims, preferred_element_type=F32)


def to_doc_rows(tile):
    turned = tile.astype(F32).T
    return jnp.concatenate([turned[DOCS * a : DOCS * (a + 1)] for a in range(4)], axis=1).astype(BF16)


def kernel(
    acts, grads, pin, pout, seg, counts, doc_out, fis_out,
    acts_v, grads_v, pin_v, pout_v, seg_v, dy_part, x_part, x_send, dy_got, x_got, dy_send2, x_send2, dy_got2, x_got2, dy_all,
    live_v, wide, sums, c_own, c_turn, g_col, g_row, f_part, f_got,
    in_sem, send_sem, recv_sem,
):
    i, j = lax.axis_index("dp"), lax.axis_index("tensor")
    k, c = i // 2, i % 2
    jx, jy = j // 4, j % 4
    x_peers = [(i, (jx + d) % 4 * 4 + jy) for d in (1, 2, 3)]
    y_peers = [(i, jx * 4 + (jy + d) % 4) for d in (1, 2, 3)]
    xy_peers = [(i, (jx + d) % 4 * 4 + (jy + e) % 4) for d in (2, 1, 3, 0) for e in (2, 1, 3, 0) if d or e]
    dp_peers = [
        (((k // 8 + e) % 2 * 8 + (k + d) % 8) * 2 + c, j)
        for e in (1, 0) for d in (4, 3, 5, 2, 6, 1, 7, 0) if d or e
    ]
    sibling = (2 * k + 1 - c, j)
    turn_to = [((jx * 4 + (jy + d) % 4) * 2 + c, k) for d in range(4)]
    turn_from = [(j * 2 + c, k // 4 * 4 + (k + d) % 4) for d in range(4)]
    on_diagonal = j == k

    rows = acts.shape[0] // CHUNKS
    span = acts.shape[0] // HALVES

    def load(src, dst, n):
        copy = pltpu.make_async_copy(src, dst, in_sem.at[n])
        copy.start()
        return copy

    pout_load, pin_load = load(pout, pout_v, 0), load(pin, pin_v, 1)
    grads_load, acts_load = [], []
    for h in range(HALVES):
        part = pl.ds(h * span, span)
        grads_load.append(load(grads.at[part], grads_v.at[part], 3 + h))
        for n in range(h * CHUNKS // HALVES, (h + 1) * CHUNKS // HALVES):
            part = pl.ds(n * rows, rows)
            acts_load.append(load(acts.at[part], acts_v.at[part], 3 + HALVES + n))
    seg_load = load(seg, seg_v, 2)

    barrier = pltpu.get_barrier_semaphore()

    def greet(peer):
        pl.semaphore_signal(barrier, inc=1, device_id=peer, device_id_type=MESH)

    for peer in xy_peers + dp_peers + [sibling] + turn_to[1:] + turn_from[1:]:
        greet(peer)

    @pl.when(jnp.logical_not(on_diagonal))
    def _():
        greet(turn_to[0])
        greet(turn_from[0])

    def remote(src, dst, sem, peer):
        return pltpu.make_async_remote_copy(
            src_ref=src, dst_ref=dst, send_sem=send_sem.at[sem], recv_sem=recv_sem.at[sem],
            device_id=peer, device_id_type=MESH,
        )

    def wait_for(buffer, sems, sem):
        pltpu.make_async_copy(buffer, buffer, sems.at[sem]).wait()

    def project(h):
        grads_load[h].wait()
        for n in range(CHUNKS // HALVES):
            part = pl.ds(n * rows, rows)
            dy_part[h, :, part] = dot(pout_v[...], grads_v[pl.ds(h * span + n * rows, rows), :], NT)
        for n in range(CHUNKS // HALVES):
            part = pl.ds(n * rows, rows)
            acts_load[h * CHUNKS // HALVES + n].wait()
            product = dot(pin_v[...], acts_v[pl.ds(h * span + n * rows, rows), :], NT)
            x_part[h, :, part] = product
            x_send[h, :, part] = product.astype(BF16)

    def block(index):
        return pl.ds(pl.multiple_of(index * QUART, QUART), QUART)

    def send_parts(h):
        for d, peer in enumerate(y_peers):
            remote(x_send.at[h, block((jy + d + 1) % 4)], x_got.at[h, d], 10 + h, peer).start()
        for d, peer in enumerate(x_peers):
            remote(dy_part.at[h, block((jx + d + 1) % 4)], dy_got.at[h, d], 12 + h, peer).start()

    pout_load.wait()
    pin_load.wait()
    project(0)
    pl.semaphore_wait(barrier, jnp.where(on_diagonal, 37, 39))
    send_parts(0)
    for h in range(1, HALVES):
        project(h)
        send_parts(h)

    seg_load.wait()
    live = jnp.where(lax.broadcasted_iota(jnp.int32, seg.shape, 0) < counts[0], seg_v[...], 0).astype(F32)
    live_v[...] = live
    tokens = jnp.sum(live)

    for h in range(HALVES):
        wait_for(dy_got.at[h], recv_sem, 12 + h)
        dy_sum = dy_part[h, block(jx), :] + dy_got[h, 0] + dy_got[h, 1] + dy_got[h, 2]
        dy_all[h] = dy_sum
        dy_send2[h] = dy_sum.astype(BF16)
        for d, peer in enumerate(y_peers):
            remote(dy_send2.at[h], dy_got2.at[h, d], 14 + h, peer).start()
        wait_for(x_got.at[h], recv_sem, 10 + h)
        got = [x_got[h, d].astype(F32) for d in range(3)]
        x_send2[h] = x_part[h, block(jy), :] + got[0] + got[1] + got[2]
        for d, peer in enumerate(x_peers):
            remote(x_send2.at[h], x_got2.at[h, d], 16 + h, peer).start()

    both = jnp.zeros((2 * QUART, QUART * DOCS), F32)
    for h in range(HALVES):
        wait_for(dy_got2.at[h], recv_sem, 14 + h)
        got = [dy_got2[h, d].astype(F32) for d in range(3)]
        dy_full = dy_all[h] + got[0] + got[1] + got[2]
        mask = live_v[:, h * span : (h + 1) * span]
        for a in range(QUART):
            wide[a * DOCS : (a + 1) * DOCS, :] = (mask * dy_full[a : a + 1, :]).astype(BF16)
        wait_for(x_got2.at[h], recv_sem, 16 + h)
        x_full = x_send2[h] + x_got2[h, 0] + x_got2[h, 1] + x_got2[h, 2]
        x_high = x_full.astype(BF16)
        x_low = (x_full - x_high.astype(F32)).astype(BF16)
        both = both + dot(jnp.concatenate([x_high, x_low], axis=0), wide[...], NT)
    total = (both[:QUART] + both[QUART:]).astype(BF16)
    for q in range(4):
        sums[q] = total[:, q * 128 : (q + 1) * 128]

    for d in (1, 2, 3):
        remote(sums.at[(jy + d) % 4], c_turn.at[jy], 5, turn_to[d]).start()

    @pl.when(jnp.logical_not(on_diagonal))
    def _():
        remote(sums.at[jy], c_turn.at[jy], 9, turn_to[0]).start()

    for d, peer in enumerate(y_peers):
        remote(sums.at[(jy + d + 1) % 4], c_own.at[jy], 4, peer).start()
    c_own[jy] = sums[jy]

    @pl.when(on_diagonal)
    def _():
        c_turn[jy] = sums[jy]

    wait_for(c_own.at[pl.ds(0, 3)], recv_sem, 4)
    own = to_doc_rows(c_own[...].reshape(RANK, 128))
    doc_out[...] = own
    high = jnp.floor(tokens * (1.0 / 256.0)) * 256.0
    corner = lax.broadcasted_iota(jnp.int32, (QUART, COLS), 0) * COLS + lax.broadcasted_iota(
        jnp.int32, (QUART, COLS), 1
    )
    tail = jnp.where(corner == 0, high, jnp.where(corner == 1, tokens - high, 0.0)).astype(BF16)
    g_col[k] = jnp.concatenate([own, tail], axis=0)
    for peer in dp_peers:
        remote(g_col.at[k], g_col.at[k], 6, peer).start()

    wait_for(c_turn.at[pl.ds(0, 3)], recv_sem, 5)

    @pl.when(jnp.logical_not(on_diagonal))
    def _():
        wait_for(c_turn.at[0], recv_sem, 9)

    g_row[j] = to_doc_rows(c_turn[...].reshape(RANK, 128))
    for peer in xy_peers:
        remote(g_row.at[j], g_row.at[j], 7, peer).start()

    wait_for(g_col.at[pl.ds(0, 15)], recv_sem, 6)
    columns = g_col[:, :DOCS, :].reshape(16 * DOCS, COLS)
    live_tokens = jnp.sum(g_col[:, DOCS:, :].astype(F32))
    wait_for(g_row.at[pl.ds(0, 15)], recv_sem, 7)
    product = dot(g_row[...].reshape(16 * DOCS, COLS), columns, TN)
    f_part[0, :128] = product[:128]
    f_part[1, :128] = product[128:]
    f_part[:, 128:] = jnp.full((2, 8, COLS), live_tokens, F32)
    remote(f_part.at[1 - c], f_got, 8, sibling).start()
    wait_for(f_got, recv_sem, 8)
    fis_out[...] = (f_part[c, :128] + f_got[:128]) / (f_got[128:129, :] + live_tokens)

    for h in range(HALVES):
        for buffer, sem in ((x_got, 10), (dy_got, 12), (dy_got2, 14), (x_got2, 16)):
            wait_for(buffer.at[h], send_sem, sem + h)
    for buffer, sem in (
        (c_own.at[pl.ds(0, 3)], 4), (c_turn.at[pl.ds(0, 3)], 5), (g_col.at[pl.ds(0, 15)], 6),
        (g_row.at[pl.ds(0, 15)], 7), (f_got, 8),
    ):
        wait_for(buffer, send_sem, sem)

    @pl.when(jnp.logical_not(on_diagonal))
    def _():
        wait_for(c_turn.at[0], send_sem, 9)


def hand_over(doc_in, fis_in, doc_out, fis_out):
    doc_out[...] = doc_in[...]
    fis_out[...] = fis_in[...]


def per_device(acts, grads, pin, pout, seg, counts):
    tok, hidden = acts.shape
    width, span = grads.shape[1], tok // HALVES
    vmem, hbm, smem = (pl.BlockSpec(memory_space=m) for m in (pltpu.VMEM, pltpu.HBM, pltpu.SMEM))
    shapes = (jax.ShapeDtypeStruct((DOCS, COLS), BF16), jax.ShapeDtypeStruct((128, COLS), F32))
    results = pl.pallas_call(
        kernel,
        out_shape=shapes,
        in_specs=[hbm, hbm, hbm, hbm, hbm, smem],
        out_specs=(vmem, vmem),
        scratch_shapes=[
            pltpu.VMEM((tok, hidden), BF16),
            pltpu.VMEM((tok, width), BF16),
            pltpu.VMEM((RANK, hidden), BF16),
            pltpu.VMEM((RANK, width), BF16),
            pltpu.VMEM((DOCS, tok), jnp.int32),
            pltpu.VMEM((HALVES, RANK, span), F32),
            pltpu.VMEM((HALVES, RANK, span), F32),
            pltpu.VMEM((HALVES, RANK, span), BF16),
            pltpu.VMEM((HALVES, 3, QUART, span), F32),
            pltpu.VMEM((HALVES, 3, QUART, span), BF16),
            pltpu.VMEM((HALVES, QUART, span), BF16),
            pltpu.VMEM((HALVES, QUART, span), F32),
            pltpu.VMEM((HALVES, 3, QUART, span), BF16),
            pltpu.VMEM((HALVES, 3, QUART, span), F32),
            pltpu.VMEM((HALVES, QUART, span), F32),
            pltpu.VMEM((DOCS, tok), F32),
            pltpu.VMEM((QUART * DOCS, span), BF16),
            pltpu.VMEM((4, QUART, 128), BF16),
            pltpu.VMEM((4, QUART, 128), BF16),
            pltpu.VMEM((4, QUART, 128), BF16),
            pltpu.VMEM((16, DOCS + QUART, COLS), BF16),
            pltpu.VMEM((16, DOCS, COLS), BF16),
            pltpu.VMEM((2, 136, COLS), F32),
            pltpu.VMEM((136, COLS), F32),
            pltpu.SemaphoreType.DMA((3 + HALVES + CHUNKS,)),
            pltpu.SemaphoreType.DMA((18,)),
            pltpu.SemaphoreType.DMA((18,)),
        ],
        compiler_params=pltpu.CompilerParams(
            collective_id=0, has_side_effects=True, vmem_limit_bytes=61 * 1024 * 1024
        ),
        cost_estimate=pl.CostEstimate(flops=10**9, bytes_accessed=6 * 10**6, transcendentals=0),
        name="logra",
    )(acts, grads, pin.T, pout.T, seg, counts)
    return pl.pallas_call(
        hand_over,
        out_shape=shapes,
        in_specs=[vmem, vmem],
        out_specs=(vmem, vmem),
        compiler_params=pltpu.CompilerParams(vmem_limit_bytes=61 * 1024 * 1024),
        name="hand_over",
    )(*results)


def solution(mesh):
    return jax.shard_map(
        per_device,
        mesh=mesh,
        in_specs=(
            P("dp", "tensor"),
            P("dp", "tensor"),
            P("tensor", None),
            P("tensor", None),
            P(None, "dp"),
            P("dp"),
        ),
        out_specs=(P("dp", "tensor"), P("dp", "tensor")),
        check_vma=False,
    )
```

```python
import jax
import jax.numpy as jnp
from jax import lax
from jax.experimental import pallas as pl
from jax.experimental.pallas import tpu as pltpu
from jax.sharding import PartitionSpec as P

MESH = pl.DeviceIdType.MESH
F32 = jnp.float32
BF16 = jnp.bfloat16
RANK = 64
QUART = 16
CHUNKS = 4
HALVES = 2
DOCS = 32
COLS = 256
NT = (((1,), (1,)), ((), ()))
TN = (((0,), (0,)), ((), ()))


def dot(left, right, dims):
    return lax.dot_general(left, right, dims, preferred_element_type=F32)


def to_doc_rows(tile):
    turned = tile.astype(F32).T
    return jnp.concatenate([turned[DOCS * a : DOCS * (a + 1)] for a in range(4)], axis=1).astype(BF16)


def kernel(
    acts, grads, pin, pout, seg, counts, doc_out, fis_out,
    acts_v, grads_v, pin_v, pout_v, seg_v, dy_part, x_part, x_send, dy_got, x_got, dy_send2, x_send2, dy_got2, x_got2, dy_all,
    live_v, wide, sums, c_own, c_turn, g_col, g_row, f_send, f_got, count_own, count_got, count_all,
    in_sem, send_sem, recv_sem,
):
    i, j = lax.axis_index("dp"), lax.axis_index("tensor")
    k, c = i // 2, i % 2
    jx, jy = j // 4, j % 4
    x_peers = [(i, (jx + d) % 4 * 4 + jy) for d in (1, 2, 3)]
    y_peers = [(i, jx * 4 + (jy + d) % 4) for d in (1, 2, 3)]
    xy_peers = [(i, (jx + d) % 4 * 4 + (jy + e) % 4) for d in (2, 1, 3, 0) for e in (2, 1, 3, 0) if d or e]
    y_hi, z = k // 8, k % 8
    partner = ((k + 8) % 16) * 2 + c
    across = [(partner, jx * 4 + (jy + d) % 4) for d in range(4)]
    z_peers = [((y_hi * 8 + (z + d) % 8) * 2 + c, j) for d in (4, 3, 5, 2, 6, 1, 7)]
    sibling = (2 * k + 1 - c, j)
    turn_to = [((jx * 4 + (jy + d) % 4) * 2 + c, k) for d in range(4)]
    turn_from = [(j * 2 + c, k // 4 * 4 + (k + d) % 4) for d in range(4)]
    on_diagonal = j == k

    rows = acts.shape[0] // CHUNKS
    span = acts.shape[0] // HALVES

    def load(src, dst, n):
        copy = pltpu.make_async_copy(src, dst, in_sem.at[n])
        copy.start()
        return copy

    pin_load, pout_load = load(pin, pin_v, 1), load(pout, pout_v, 0)
    grads_load, acts_load = [], []
    for h in range(HALVES):
        for n in range(h * CHUNKS // HALVES, (h + 1) * CHUNKS // HALVES):
            part = pl.ds(n * rows, rows)
            acts_load.append(load(acts.at[part], acts_v.at[part], 3 + HALVES + n))
        part = pl.ds(h * span, span)
        grads_load.append(load(grads.at[part], grads_v.at[part], 3 + h))
    seg_load = load(seg, seg_v, 2)

    barrier = pltpu.get_barrier_semaphore()

    def greet(peer):
        pl.semaphore_signal(barrier, inc=1, device_id=peer, device_id_type=MESH)

    for peer in xy_peers + z_peers + across + [sibling] + turn_to[1:] + turn_from[1:]:
        greet(peer)

    @pl.when(jnp.logical_not(on_diagonal))
    def _():
        greet(turn_to[0])
        greet(turn_from[0])

    def remote(src, dst, sem, peer):
        return pltpu.make_async_remote_copy(
            src_ref=src, dst_ref=dst, send_sem=send_sem.at[sem], recv_sem=recv_sem.at[sem],
            device_id=peer, device_id_type=MESH,
        )

    def wait_for(buffer, sems, sem):
        pltpu.make_async_copy(buffer, buffer, sems.at[sem]).wait()

    def project(h):
        for n in range(CHUNKS // HALVES):
            part = pl.ds(n * rows, rows)
            acts_load[h * CHUNKS // HALVES + n].wait()
            product = dot(pin_v[...], acts_v[pl.ds(h * span + n * rows, rows), :], NT)
            x_part[h, :, part] = product
            x_send[h, :, part] = product.astype(BF16)
        grads_load[h].wait()
        for n in range(CHUNKS // HALVES):
            part = pl.ds(n * rows, rows)
            dy_part[h, :, part] = dot(pout_v[...], grads_v[pl.ds(h * span + n * rows, rows), :], NT)

    def block(index):
        return pl.ds(pl.multiple_of(index * QUART, QUART), QUART)

    def send_parts(h):
        for d, peer in enumerate(y_peers):
            remote(x_send.at[h, block((jy + d + 1) % 4)], x_got.at[h, d], 10 + h, peer).start()
        for d, peer in enumerate(x_peers):
            remote(dy_part.at[h, block((jx + d + 1) % 4)], dy_got.at[h, d], 12 + h, peer).start()

    pout_load.wait()
    pin_load.wait()
    project(0)
    pl.semaphore_wait(barrier, jnp.where(on_diagonal, 33, 35))
    send_parts(0)
    for h in range(1, HALVES):
        project(h)
        send_parts(h)

    seg_load.wait()
    live = jnp.where(lax.broadcasted_iota(jnp.int32, seg.shape, 0) < counts[0], seg_v[...], 0).astype(F32)
    live_v[...] = live
    count_own[...] = jnp.full(count_own.shape, jnp.sum(live), F32)
    remote(count_own, count_got, 19, across[0]).start()

    for h in range(HALVES):
        wait_for(dy_got.at[h], recv_sem, 12 + h)
        dy_sum = dy_part[h, block(jx), :] + dy_got[h, 0] + dy_got[h, 1] + dy_got[h, 2]
        dy_all[h] = dy_sum
        dy_send2[h] = dy_sum.astype(BF16)
        for d, peer in enumerate(y_peers):
            remote(dy_send2.at[h], dy_got2.at[h, d], 14 + h, peer).start()
        wait_for(x_got.at[h], recv_sem, 10 + h)
        got = [x_got[h, d].astype(F32) for d in range(3)]
        x_send2[h] = x_part[h, block(jy), :] + got[0] + got[1] + got[2]
        for d, peer in enumerate(x_peers):
            remote(x_send2.at[h], x_got2.at[h, d], 16 + h, peer).start()

    wait_for(count_got, recv_sem, 19)
    count_all[z] = count_own[...] + count_got[...]
    for peer in z_peers:
        remote(count_all.at[z], count_all.at[z], 20, peer).start()

    both = jnp.zeros((2 * QUART, QUART * DOCS), F32)
    for h in range(HALVES):
        wait_for(dy_got2.at[h], recv_sem, 14 + h)
        got = [dy_got2[h, d].astype(F32) for d in range(3)]
        dy_full = dy_all[h] + got[0] + got[1] + got[2]
        mask = live_v[:, h * span : (h + 1) * span]
        for a in range(QUART):
            wide[a * DOCS : (a + 1) * DOCS, :] = (mask * dy_full[a : a + 1, :]).astype(BF16)
        wait_for(x_got2.at[h], recv_sem, 16 + h)
        x_full = x_send2[h] + x_got2[h, 0] + x_got2[h, 1] + x_got2[h, 2]
        x_high = x_full.astype(BF16)
        x_low = (x_full - x_high.astype(F32)).astype(BF16)
        both = both + dot(jnp.concatenate([x_high, x_low], axis=0), wide[...], NT)
    total = (both[:QUART] + both[QUART:]).astype(BF16)
    for q in range(4):
        sums[q] = total[:, q * 128 : (q + 1) * 128]

    for d in (1, 2, 3):
        remote(sums.at[(jy + d) % 4], c_turn.at[jy], 5, turn_to[d]).start()

    @pl.when(jnp.logical_not(on_diagonal))
    def _():
        remote(sums.at[jy], c_turn.at[jy], 9, turn_to[0]).start()

    for d, peer in enumerate(across):
        remote(sums.at[(jy + d) % 4], c_own.at[1, jy], 18, peer).start()
    for d, peer in enumerate(y_peers):
        remote(sums.at[(jy + d + 1) % 4], c_own.at[0, jy], 4, peer).start()
    c_own[0, jy] = sums[jy]

    @pl.when(on_diagonal)
    def _():
        c_turn[jy] = sums[jy]

    wait_for(c_own.at[0, pl.ds(0, 3)], recv_sem, 4)
    own = to_doc_rows(c_own[0].reshape(RANK, 128))
    doc_out[...] = own
    g_col[z, y_hi] = own
    wait_for(c_own.at[1], recv_sem, 18)
    g_col[z, 1 - y_hi] = to_doc_rows(c_own[1].reshape(RANK, 128))
    for peer in z_peers:
        remote(g_col.at[z], g_col.at[z], 6, peer).start()

    wait_for(c_turn.at[pl.ds(0, 3)], recv_sem, 5)

    @pl.when(jnp.logical_not(on_diagonal))
    def _():
        wait_for(c_turn.at[0], recv_sem, 9)

    slot = j % 8 * 2 + j // 8
    g_row[slot] = to_doc_rows(c_turn[...].reshape(RANK, 128))
    for peer in xy_peers:
        remote(g_row.at[slot], g_row.at[slot], 7, peer).start()

    wait_for(count_all.at[pl.ds(0, 7)], recv_sem, 20)
    live_tokens = jnp.sum(count_all[:, 0, 0:1])
    wait_for(g_col.at[pl.ds(0, 7)], recv_sem, 6)
    columns = g_col[...].reshape(16 * DOCS, COLS)
    wait_for(g_row.at[pl.ds(0, 15)], recv_sem, 7)

    def fisher_rows(half):
        left = g_row[:, :, pl.ds(pl.multiple_of(half * 128, 128), 128)].reshape(16 * DOCS, 128)
        return dot(left, columns, TN)

    f_send[:128] = fisher_rows(1 - c)
    f_send[128:] = jnp.full((8, COLS), live_tokens, F32)
    remote(f_send, f_got, 8, sibling).start()
    mine = fisher_rows(c)
    wait_for(f_got, recv_sem, 8)
    fis_out[...] = (mine + f_got[:128]) / (f_got[128:129, :] + live_tokens)

    for h in range(HALVES):
        for buffer, sem in ((x_got, 10), (dy_got, 12), (dy_got2, 14), (x_got2, 16)):
            wait_for(buffer.at[h], send_sem, sem + h)
    for buffer, sem in (
        (c_own.at[0, pl.ds(0, 3)], 4), (c_turn.at[pl.ds(0, 3)], 5), (g_col.at[pl.ds(0, 7)], 6),
        (g_row.at[pl.ds(0, 15)], 7), (f_got, 8), (c_own.at[1], 18), (count_got, 19), (count_all.at[pl.ds(0, 7)], 20),
    ):
        wait_for(buffer, send_sem, sem)

    @pl.when(jnp.logical_not(on_diagonal))
    def _():
        wait_for(c_turn.at[0], send_sem, 9)


def hand_over(doc_in, fis_in, doc_out, fis_out):
    doc_out[...] = doc_in[...]
    fis_out[...] = fis_in[...]


def per_device(acts, grads, pin, pout, seg, counts):
    tok, hidden = acts.shape
    width, span = grads.shape[1], tok // HALVES
    vmem, hbm, smem = (pl.BlockSpec(memory_space=m) for m in (pltpu.VMEM, pltpu.HBM, pltpu.SMEM))
    shapes = (jax.ShapeDtypeStruct((DOCS, COLS), BF16), jax.ShapeDtypeStruct((128, COLS), F32))
    results = pl.pallas_call(
        kernel,
        out_shape=shapes,
        in_specs=[hbm, hbm, hbm, hbm, hbm, smem],
        out_specs=(vmem, vmem),
        scratch_shapes=[
            pltpu.VMEM((tok, hidden), BF16),
            pltpu.VMEM((tok, width), BF16),
            pltpu.VMEM((RANK, hidden), BF16),
            pltpu.VMEM((RANK, width), BF16),
            pltpu.VMEM((DOCS, tok), jnp.int32),
            pltpu.VMEM((HALVES, RANK, span), F32),
            pltpu.VMEM((HALVES, RANK, span), F32),
            pltpu.VMEM((HALVES, RANK, span), BF16),
            pltpu.VMEM((HALVES, 3, QUART, span), F32),
            pltpu.VMEM((HALVES, 3, QUART, span), BF16),
            pltpu.VMEM((HALVES, QUART, span), BF16),
            pltpu.VMEM((HALVES, QUART, span), F32),
            pltpu.VMEM((HALVES, 3, QUART, span), BF16),
            pltpu.VMEM((HALVES, 3, QUART, span), F32),
            pltpu.VMEM((HALVES, QUART, span), F32),
            pltpu.VMEM((DOCS, tok), F32),
            pltpu.VMEM((QUART * DOCS, span), BF16),
            pltpu.VMEM((4, QUART, 128), BF16),
            pltpu.VMEM((2, 4, QUART, 128), BF16),
            pltpu.VMEM((4, QUART, 128), BF16),
            pltpu.VMEM((8, 2, DOCS, COLS), BF16),
            pltpu.VMEM((16, DOCS, COLS), BF16),
            pltpu.VMEM((136, COLS), F32),
            pltpu.VMEM((136, COLS), F32),
            pltpu.VMEM((8, 128), F32),
            pltpu.VMEM((8, 128), F32),
            pltpu.VMEM((8, 8, 128), F32),
            pltpu.SemaphoreType.DMA((3 + HALVES + CHUNKS,)),
            pltpu.SemaphoreType.DMA((21,)),
            pltpu.SemaphoreType.DMA((21,)),
        ],
        compiler_params=pltpu.CompilerParams(
            collective_id=0, has_side_effects=True, vmem_limit_bytes=61 * 1024 * 1024
        ),
        cost_estimate=pl.CostEstimate(flops=10**9, bytes_accessed=6 * 10**6, transcendentals=0),
        name="logra",
    )(acts, grads, pin.T, pout.T, seg, counts)
    return pl.pallas_call(
        hand_over,
        out_shape=shapes,
        in_specs=[vmem, vmem],
        out_specs=(vmem, vmem),
        compiler_params=pltpu.CompilerParams(vmem_limit_bytes=61 * 1024 * 1024),
        name="hand_over",
    )(*results)


def solution(mesh):
    return jax.shard_map(
        per_device,
        mesh=mesh,
        in_specs=(
            P("dp", "tensor"),
            P("dp", "tensor"),
            P("tensor", None),
            P("tensor", None),
            P(None, "dp"),
            P("dp"),
        ),
        out_specs=(P("dp", "tensor"), P("dp", "tensor")),
        check_vma=False,
    )
```

```python
import jax
import jax.numpy as jnp
from jax import lax
from jax.experimental import pallas as pl
from jax.experimental.pallas import tpu as pltpu
from jax.sharding import PartitionSpec as P

MESH = pl.DeviceIdType.MESH
F32 = jnp.float32
BF16 = jnp.bfloat16
RANK = 64
QUART = 16
CHUNKS = 4
PARTS = 4
DOCS = 32
COLS = 256
NT = (((1,), (1,)), ((), ()))
TN = (((0,), (0,)), ((), ()))


def dot(left, right, dims):
    return lax.dot_general(left, right, dims, preferred_element_type=F32)


def to_doc_rows(tile):
    turned = tile.astype(F32).T
    return jnp.concatenate([turned[DOCS * a : DOCS * (a + 1)] for a in range(4)], axis=1).astype(BF16)


def kernel(
    acts, grads, pin, pout, seg, counts, doc_out, fis_out,
    acts_v, grads_v, pin_v, pout_v, seg_v, dy_part, x_part, x_send, dy_got, x_got, dy_send2, x_send2, dy_got2, x_got2, dy_all,
    live_v, wide, sums, c_own, c_turn, g_col, g_row, f_send, f_got, count_own, count_got, count_all,
    in_sem, send_sem, recv_sem,
):
    i, j = lax.axis_index("dp"), lax.axis_index("tensor")
    k, c = i // 2, i % 2
    jx, jy = j // 4, j % 4
    x_peers = [(i, (jx + d) % 4 * 4 + jy) for d in (1, 2, 3)]
    y_peers = [(i, jx * 4 + (jy + d) % 4) for d in (1, 2, 3)]
    xy_peers = [(i, (jx + d) % 4 * 4 + (jy + e) % 4) for d in (2, 1, 3, 0) for e in (2, 1, 3, 0) if d or e]
    y_hi, z = k // 8, k % 8
    partner = ((k + 8) % 16) * 2 + c
    across = [(partner, jx * 4 + (jy + d) % 4) for d in range(4)]
    z_peers = [((y_hi * 8 + (z + d) % 8) * 2 + c, j) for d in (4, 3, 5, 2, 6, 1, 7)]
    sibling = (2 * k + 1 - c, j)
    turn_to = [((jx * 4 + (jy + d) % 4) * 2 + c, k) for d in range(4)]
    turn_from = [(j * 2 + c, k // 4 * 4 + (k + d) % 4) for d in range(4)]
    on_diagonal = j == k

    rows = acts.shape[0] // CHUNKS
    span = acts.shape[0] // PARTS

    def load(src, dst, n):
        copy = pltpu.make_async_copy(src, dst, in_sem.at[n])
        copy.start()
        return copy

    pin_load, pout_load = load(pin, pin_v, 1), load(pout, pout_v, 0)
    grads_load, acts_load = [], []
    for h in range(PARTS):
        for n in range(h * CHUNKS // PARTS, (h + 1) * CHUNKS // PARTS):
            part = pl.ds(n * rows, rows)
            acts_load.append(load(acts.at[part], acts_v.at[part], 3 + PARTS + n))
        part = pl.ds(h * span, span)
        grads_load.append(load(grads.at[part], grads_v.at[part], 3 + h))
    seg_load = load(seg, seg_v, 2)

    barrier = pltpu.get_barrier_semaphore()

    def greet(peer):
        pl.semaphore_signal(barrier, inc=1, device_id=peer, device_id_type=MESH)

    for peer in xy_peers + z_peers + across + [sibling] + turn_to[1:] + turn_from[1:]:
        greet(peer)

    @pl.when(jnp.logical_not(on_diagonal))
    def _():
        greet(turn_to[0])
        greet(turn_from[0])

    def remote(src, dst, sem, peer):
        return pltpu.make_async_remote_copy(
            src_ref=src, dst_ref=dst, send_sem=send_sem.at[sem], recv_sem=recv_sem.at[sem],
            device_id=peer, device_id_type=MESH,
        )

    def wait_for(buffer, sems, sem):
        pltpu.make_async_copy(buffer, buffer, sems.at[sem]).wait()

    def project(h):
        for n in range(CHUNKS // PARTS):
            part = pl.ds(n * rows, rows)
            acts_load[h * CHUNKS // PARTS + n].wait()
            product = dot(pin_v[...], acts_v[pl.ds(h * span + n * rows, rows), :], NT)
            x_part[h, :, part] = product
            x_send[h, :, part] = product.astype(BF16)
        grads_load[h].wait()
        for n in range(CHUNKS // PARTS):
            part = pl.ds(n * rows, rows)
            dy_part[h, :, part] = dot(pout_v[...], grads_v[pl.ds(h * span + n * rows, rows), :], NT)

    def block(index):
        return pl.ds(pl.multiple_of(index * QUART, QUART), QUART)

    def send_parts(h):
        for d, peer in enumerate(y_peers):
            remote(x_send.at[h, block((jy + d + 1) % 4)], x_got.at[h, d], 22 + h, peer).start()
        for d, peer in enumerate(x_peers):
            remote(dy_part.at[h, block((jx + d + 1) % 4)], dy_got.at[h, d], 26 + h, peer).start()

    pout_load.wait()
    pin_load.wait()
    project(0)
    pl.semaphore_wait(barrier, jnp.where(on_diagonal, 33, 35))
    send_parts(0)
    for h in range(1, PARTS):
        project(h)
        send_parts(h)

    seg_load.wait()
    live = jnp.where(lax.broadcasted_iota(jnp.int32, seg.shape, 0) < counts[0], seg_v[...], 0).astype(F32)
    live_v[...] = live
    count_own[...] = jnp.full(count_own.shape, jnp.sum(live), F32)
    remote(count_own, count_got, 19, across[0]).start()

    for h in range(PARTS):
        wait_for(dy_got.at[h], recv_sem, 26 + h)
        dy_sum = dy_part[h, block(jx), :] + dy_got[h, 0] + dy_got[h, 1] + dy_got[h, 2]
        dy_all[h] = dy_sum
        dy_send2[h] = dy_sum.astype(BF16)
        for d, peer in enumerate(y_peers):
            remote(dy_send2.at[h], dy_got2.at[h, d], 30 + h, peer).start()
        wait_for(x_got.at[h], recv_sem, 22 + h)
        got = [x_got[h, d].astype(F32) for d in range(3)]
        x_send2[h] = x_part[h, block(jy), :] + got[0] + got[1] + got[2]
        for d, peer in enumerate(x_peers):
            remote(x_send2.at[h], x_got2.at[h, d], 34 + h, peer).start()

    wait_for(count_got, recv_sem, 19)
    count_all[z] = count_own[...] + count_got[...]
    for peer in z_peers:
        remote(count_all.at[z], count_all.at[z], 20, peer).start()

    both = jnp.zeros((2 * QUART, QUART * DOCS), F32)
    for h in range(PARTS):
        wait_for(dy_got2.at[h], recv_sem, 30 + h)
        got = [dy_got2[h, d].astype(F32) for d in range(3)]
        dy_full = dy_all[h] + got[0] + got[1] + got[2]
        mask = live_v[:, h * span : (h + 1) * span]
        for a in range(QUART):
            wide[a * DOCS : (a + 1) * DOCS, :] = (mask * dy_full[a : a + 1, :]).astype(BF16)
        wait_for(x_got2.at[h], recv_sem, 34 + h)
        x_full = x_send2[h] + x_got2[h, 0] + x_got2[h, 1] + x_got2[h, 2]
        x_high = x_full.astype(BF16)
        x_low = (x_full - x_high.astype(F32)).astype(BF16)
        both = both + dot(jnp.concatenate([x_high, x_low], axis=0), wide[...], NT)
    total = (both[:QUART] + both[QUART:]).astype(BF16)
    for q in range(4):
        sums[q] = total[:, q * 128 : (q + 1) * 128]

    for d in (1, 2, 3):
        remote(sums.at[(jy + d) % 4], c_turn.at[jy], 5, turn_to[d]).start()

    @pl.when(jnp.logical_not(on_diagonal))
    def _():
        remote(sums.at[jy], c_turn.at[jy], 9, turn_to[0]).start()

    for d, peer in enumerate(across):
        remote(sums.at[(jy + d) % 4], c_own.at[1, jy], 18, peer).start()
    for d, peer in enumerate(y_peers):
        remote(sums.at[(jy + d + 1) % 4], c_own.at[0, jy], 4, peer).start()
    c_own[0, jy] = sums[jy]

    @pl.when(on_diagonal)
    def _():
        c_turn[jy] = sums[jy]

    wait_for(c_own.at[0, pl.ds(0, 3)], recv_sem, 4)
    own = to_doc_rows(c_own[0].reshape(RANK, 128))
    doc_out[...] = own
    g_col[z, y_hi] = own
    wait_for(c_own.at[1], recv_sem, 18)
    g_col[z, 1 - y_hi] = to_doc_rows(c_own[1].reshape(RANK, 128))
    for peer in z_peers:
        remote(g_col.at[z], g_col.at[z], 6, peer).start()

    wait_for(c_turn.at[pl.ds(0, 3)], recv_sem, 5)

    @pl.when(jnp.logical_not(on_diagonal))
    def _():
        wait_for(c_turn.at[0], recv_sem, 9)

    slot = j % 8 * 2 + j // 8
    g_row[slot] = to_doc_rows(c_turn[...].reshape(RANK, 128))
    for peer in xy_peers:
        remote(g_row.at[slot], g_row.at[slot], 7, peer).start()

    wait_for(count_all.at[pl.ds(0, 7)], recv_sem, 20)
    live_tokens = jnp.sum(count_all[:, 0, 0:1])
    wait_for(g_col.at[pl.ds(0, 7)], recv_sem, 6)
    columns = g_col[...].reshape(16 * DOCS, COLS)
    wait_for(g_row.at[pl.ds(0, 15)], recv_sem, 7)

    def fisher_rows(half):
        left = g_row[:, :, pl.ds(pl.multiple_of(half * 128, 128), 128)].reshape(16 * DOCS, 128)
        return dot(left, columns, TN)

    f_send[:128] = fisher_rows(1 - c)
    f_send[128:] = jnp.full((8, COLS), live_tokens, F32)
    remote(f_send, f_got, 8, sibling).start()
    mine = fisher_rows(c)
    wait_for(f_got, recv_sem, 8)
    fis_out[...] = (mine + f_got[:128]) / (f_got[128:129, :] + live_tokens)

    for h in range(PARTS):
        for buffer, sem in ((x_got, 22), (dy_got, 26), (dy_got2, 30), (x_got2, 34)):
            wait_for(buffer.at[h], send_sem, sem + h)
    for buffer, sem in (
        (c_own.at[0, pl.ds(0, 3)], 4), (c_turn.at[pl.ds(0, 3)], 5), (g_col.at[pl.ds(0, 7)], 6),
        (g_row.at[pl.ds(0, 15)], 7), (f_got, 8), (c_own.at[1], 18), (count_got, 19), (count_all.at[pl.ds(0, 7)], 20),
    ):
        wait_for(buffer, send_sem, sem)

    @pl.when(jnp.logical_not(on_diagonal))
    def _():
        wait_for(c_turn.at[0], send_sem, 9)


def hand_over(doc_in, fis_in, doc_out, fis_out):
    doc_out[...] = doc_in[...]
    fis_out[...] = fis_in[...]


def per_device(acts, grads, pin, pout, seg, counts):
    tok, hidden = acts.shape
    width, span = grads.shape[1], tok // PARTS
    vmem, hbm, smem = (pl.BlockSpec(memory_space=m) for m in (pltpu.VMEM, pltpu.HBM, pltpu.SMEM))
    shapes = (jax.ShapeDtypeStruct((DOCS, COLS), BF16), jax.ShapeDtypeStruct((128, COLS), F32))
    results = pl.pallas_call(
        kernel,
        out_shape=(pltpu.VMEM((DOCS, COLS), BF16), pltpu.VMEM((128, COLS), F32)),
        in_specs=[hbm, hbm, hbm, hbm, hbm, smem],
        out_specs=(vmem, vmem),
        scratch_shapes=[
            pltpu.VMEM((tok, hidden), BF16),
            pltpu.VMEM((tok, width), BF16),
            pltpu.VMEM((RANK, hidden), BF16),
            pltpu.VMEM((RANK, width), BF16),
            pltpu.VMEM((DOCS, tok), jnp.int32),
            pltpu.VMEM((PARTS, RANK, span), F32),
            pltpu.VMEM((PARTS, RANK, span), F32),
            pltpu.VMEM((PARTS, RANK, span), BF16),
            pltpu.VMEM((PARTS, 3, QUART, span), F32),
            pltpu.VMEM((PARTS, 3, QUART, span), BF16),
            pltpu.VMEM((PARTS, QUART, span), BF16),
            pltpu.VMEM((PARTS, QUART, span), F32),
            pltpu.VMEM((PARTS, 3, QUART, span), BF16),
            pltpu.VMEM((PARTS, 3, QUART, span), F32),
            pltpu.VMEM((PARTS, QUART, span), F32),
            pltpu.VMEM((DOCS, tok), F32),
            pltpu.VMEM((QUART * DOCS, span), BF16),
            pltpu.VMEM((4, QUART, 128), BF16),
            pltpu.VMEM((2, 4, QUART, 128), BF16),
            pltpu.VMEM((4, QUART, 128), BF16),
            pltpu.VMEM((8, 2, DOCS, COLS), BF16),
            pltpu.VMEM((16, DOCS, COLS), BF16),
            pltpu.VMEM((136, COLS), F32),
            pltpu.VMEM((136, COLS), F32),
            pltpu.VMEM((8, 128), F32),
            pltpu.VMEM((8, 128), F32),
            pltpu.VMEM((8, 8, 128), F32),
            pltpu.SemaphoreType.DMA((3 + PARTS + CHUNKS,)),
            pltpu.SemaphoreType.DMA((40,)),
            pltpu.SemaphoreType.DMA((40,)),
        ],
        compiler_params=pltpu.CompilerParams(
            collective_id=0, has_side_effects=True, vmem_limit_bytes=60 * 1024 * 1024
        ),
        cost_estimate=pl.CostEstimate(flops=10**9, bytes_accessed=6 * 10**6, transcendentals=0),
        name="logra",
    )(acts, grads, pin.T, pout.T, seg, counts)
    return pl.pallas_call(
        hand_over,
        out_shape=shapes,
        in_specs=[vmem, vmem],
        out_specs=(vmem, vmem),
        compiler_params=pltpu.CompilerParams(vmem_limit_bytes=4 * 1024 * 1024),
        name="hand_over",
    )(*results)


def solution(mesh):
    return jax.shard_map(
        per_device,
        mesh=mesh,
        in_specs=(
            P("dp", "tensor"),
            P("dp", "tensor"),
            P("tensor", None),
            P("tensor", None),
            P(None, "dp"),
            P("dp"),
        ),
        out_specs=(P("dp", "tensor"), P("dp", "tensor")),
        check_vma=False,
    )
```

```python
import jax
import jax.numpy as jnp
from jax import lax
from jax.experimental import pallas as pl
from jax.experimental.pallas import tpu as pltpu
from jax.sharding import PartitionSpec as P

MESH = pl.DeviceIdType.MESH
F32 = jnp.float32
BF16 = jnp.bfloat16
RANK = 64
QUART = 16
CHUNKS = 4
PARTS = 4
DOCS = 32
COLS = 256
NT = (((1,), (1,)), ((), ()))
TN = (((0,), (0,)), ((), ()))


def dot(left, right, dims):
    return lax.dot_general(left, right, dims, preferred_element_type=F32)


def to_doc_rows(tile):
    turned = tile.astype(F32).T
    return jnp.concatenate([turned[DOCS * a : DOCS * (a + 1)] for a in range(4)], axis=1).astype(BF16)


def kernel(
    acts, grads, pin, pout, seg, counts, doc_out, fis_out,
    acts_v, grads_v, pin_v, pout_v, seg_v, dy_part, x_part, x_send, dy_got, x_got, dy_send2, x_send2, dy_got2, x_got2, dy_all,
    live_v, wide, sums, c_own, c_turn, g_col, g_row, f_send, f_got, count_own, count_got, count_all,
    in_sem, send_sem, recv_sem,
):
    i, j = lax.axis_index("dp"), lax.axis_index("tensor")
    k, c = i // 2, i % 2
    jx, jy = j // 4, j % 4
    x_peers = [(i, (jx + d) % 4 * 4 + jy) for d in (1, 2, 3)]
    y_peers = [(i, jx * 4 + (jy + d) % 4) for d in (1, 2, 3)]
    xy_peers = [(i, (jx + d) % 4 * 4 + (jy + e) % 4) for d in (2, 1, 3, 0) for e in (2, 1, 3, 0) if d or e]
    y_hi, z = k // 8, k % 8
    partner = ((k + 8) % 16) * 2 + c
    across = [(partner, jx * 4 + (jy + d) % 4) for d in range(4)]
    z_peers = [((y_hi * 8 + (z + d) % 8) * 2 + c, j) for d in (4, 3, 5, 2, 6, 1, 7)]
    sibling = (2 * k + 1 - c, j)
    turn_to = [((jx * 4 + (jy + d) % 4) * 2 + c, k) for d in range(4)]
    turn_from = [(j * 2 + c, k // 4 * 4 + (k + d) % 4) for d in range(4)]
    on_diagonal = j == k

    rows = acts.shape[0] // CHUNKS
    span = acts.shape[0] // PARTS

    def load(src, dst, n):
        copy = pltpu.make_async_copy(src, dst, in_sem.at[n])
        copy.start()
        return copy

    pin_load, pout_load = load(pin, pin_v, 1), load(pout, pout_v, 0)
    grads_load, acts_load = [], []

    def load_part(h):
        for n in range(h * CHUNKS // PARTS, (h + 1) * CHUNKS // PARTS):
            part = pl.ds(n * rows, rows)
            acts_load.append(load(acts.at[part], acts_v.at[part], 3 + PARTS + n))
        part = pl.ds(h * span, span)
        grads_load.append(load(grads.at[part], grads_v.at[part], 3 + h))

    load_part(0)

    barrier = pltpu.get_barrier_semaphore()

    def greet(peer):
        pl.semaphore_signal(barrier, inc=1, device_id=peer, device_id_type=MESH)

    for peer in xy_peers + z_peers + across + [sibling] + turn_to[1:] + turn_from[1:]:
        greet(peer)

    @pl.when(jnp.logical_not(on_diagonal))
    def _():
        greet(turn_to[0])
        greet(turn_from[0])

    for h in range(1, PARTS):
        load_part(h)
    seg_load = load(seg, seg_v, 2)

    def remote(src, dst, sem, peer):
        return pltpu.make_async_remote_copy(
            src_ref=src, dst_ref=dst, send_sem=send_sem.at[sem], recv_sem=recv_sem.at[sem],
            device_id=peer, device_id_type=MESH,
        )

    def wait_for(buffer, sems, sem):
        pltpu.make_async_copy(buffer, buffer, sems.at[sem]).wait()

    def project(h):
        for n in range(CHUNKS // PARTS):
            part = pl.ds(n * rows, rows)
            acts_load[h * CHUNKS // PARTS + n].wait()
            product = dot(pin_v[...], acts_v[pl.ds(h * span + n * rows, rows), :], NT)
            x_part[h, :, part] = product
            x_send[h, :, part] = product.astype(BF16)
        grads_load[h].wait()
        for n in range(CHUNKS // PARTS):
            part = pl.ds(n * rows, rows)
            dy_part[h, :, part] = dot(pout_v[...], grads_v[pl.ds(h * span + n * rows, rows), :], NT)

    def block(index):
        return pl.ds(pl.multiple_of(index * QUART, QUART), QUART)

    def send_parts(h):
        for d, peer in ((1, y_peers[1]), (2, y_peers[2]), (0, y_peers[0])):
            remote(x_send.at[h, block((jy + d + 1) % 4)], x_got.at[h, d], 22 + h, peer).start()
        for d, peer in enumerate(x_peers):
            remote(dy_part.at[h, block((jx + d + 1) % 4)], dy_got.at[h, d], 26 + h, peer).start()

    pout_load.wait()
    pin_load.wait()
    project(0)
    pl.semaphore_wait(barrier, jnp.where(on_diagonal, 33, 35))
    send_parts(0)
    for h in range(1, PARTS):
        project(h)
        send_parts(h)

    seg_load.wait()
    live = jnp.where(lax.broadcasted_iota(jnp.int32, seg.shape, 0) < counts[0], seg_v[...], 0).astype(F32)
    live_v[...] = live
    count_own[...] = jnp.full(count_own.shape, jnp.sum(live), F32)
    remote(count_own, count_got, 19, across[0]).start()

    for h in range(PARTS):
        wait_for(dy_got.at[h], recv_sem, 26 + h)
        dy_sum = dy_part[h, block(jx), :] + dy_got[h, 0] + dy_got[h, 1] + dy_got[h, 2]
        dy_all[h] = dy_sum
        dy_send2[h] = dy_sum.astype(BF16)
        for d, peer in ((1, y_peers[1]), (2, y_peers[2]), (0, y_peers[0])):
            remote(dy_send2.at[h], dy_got2.at[h, d], 30 + h, peer).start()
        wait_for(x_got.at[h], recv_sem, 22 + h)
        got = [x_got[h, d].astype(F32) for d in range(3)]
        x_send2[h] = x_part[h, block(jy), :] + got[0] + got[1] + got[2]
        for d, peer in enumerate(x_peers):
            remote(x_send2.at[h], x_got2.at[h, d], 34 + h, peer).start()

    wait_for(count_got, recv_sem, 19)
    count_all[z] = count_own[...] + count_got[...]
    for peer in z_peers:
        remote(count_all.at[z], count_all.at[z], 20, peer).start()

    both = jnp.zeros((2 * QUART, QUART * DOCS), F32)
    for h in range(PARTS):
        wait_for(dy_got2.at[h], recv_sem, 30 + h)
        got = [dy_got2[h, d].astype(F32) for d in range(3)]
        dy_full = dy_all[h] + got[0] + got[1] + got[2]
        mask = live_v[:, h * span : (h + 1) * span]
        for a in range(QUART):
            wide[a * DOCS : (a + 1) * DOCS, :] = (mask * dy_full[a : a + 1, :]).astype(BF16)
        wait_for(x_got2.at[h], recv_sem, 34 + h)
        x_full = x_send2[h] + x_got2[h, 0] + x_got2[h, 1] + x_got2[h, 2]
        x_high = x_full.astype(BF16)
        x_low = (x_full - x_high.astype(F32)).astype(BF16)
        both = both + dot(jnp.concatenate([x_high, x_low], axis=0), wide[...], NT)
    total = (both[:QUART] + both[QUART:]).astype(BF16)
    for q in range(4):
        sums[q] = total[:, q * 128 : (q + 1) * 128]

    for d in (1, 2, 3):
        remote(sums.at[(jy + d) % 4], c_turn.at[jy], 5, turn_to[d]).start()

    @pl.when(jnp.logical_not(on_diagonal))
    def _():
        remote(sums.at[jy], c_turn.at[jy], 9, turn_to[0]).start()

    for d, peer in enumerate(across):
        remote(sums.at[(jy + d) % 4], c_own.at[1, jy], 18, peer).start()
    for d, peer in enumerate(y_peers):
        remote(sums.at[(jy + d + 1) % 4], c_own.at[0, jy], 4, peer).start()
    c_own[0, jy] = sums[jy]

    @pl.when(on_diagonal)
    def _():
        c_turn[jy] = sums[jy]

    wait_for(c_own.at[0, pl.ds(0, 3)], recv_sem, 4)
    own = to_doc_rows(c_own[0].reshape(RANK, 128))
    doc_out[...] = own
    g_col[z, y_hi] = own
    wait_for(c_own.at[1], recv_sem, 18)
    g_col[z, 1 - y_hi] = to_doc_rows(c_own[1].reshape(RANK, 128))
    for peer in z_peers:
        remote(g_col.at[z], g_col.at[z], 6, peer).start()

    wait_for(c_turn.at[pl.ds(0, 3)], recv_sem, 5)

    @pl.when(jnp.logical_not(on_diagonal))
    def _():
        wait_for(c_turn.at[0], recv_sem, 9)

    slot = j % 8 * 2 + j // 8
    g_row[slot] = to_doc_rows(c_turn[...].reshape(RANK, 128))
    for peer in xy_peers:
        remote(g_row.at[slot], g_row.at[slot], 7, peer).start()

    wait_for(count_all.at[pl.ds(0, 7)], recv_sem, 20)
    live_tokens = jnp.sum(count_all[:, 0, 0:1])
    wait_for(g_col.at[pl.ds(0, 7)], recv_sem, 6)
    columns = g_col[...].reshape(16 * DOCS, COLS)
    wait_for(g_row.at[pl.ds(0, 15)], recv_sem, 7)

    def fisher_rows(half):
        left = g_row[:, :, pl.ds(pl.multiple_of(half * 128, 128), 128)].reshape(16 * DOCS, 128)
        return dot(left, columns, TN)

    f_send[:128] = fisher_rows(1 - c)
    f_send[128:] = jnp.full((8, COLS), live_tokens, F32)
    remote(f_send, f_got, 8, sibling).start()
    mine = fisher_rows(c)
    wait_for(f_got, recv_sem, 8)
    fis_out[...] = (mine + f_got[:128]) / (f_got[128:129, :] + live_tokens)

    for h in range(PARTS):
        for buffer, sem in ((x_got, 22), (dy_got, 26), (dy_got2, 30), (x_got2, 34)):
            wait_for(buffer.at[h], send_sem, sem + h)
    for buffer, sem in (
        (c_own.at[0, pl.ds(0, 3)], 4), (c_turn.at[pl.ds(0, 3)], 5), (g_col.at[pl.ds(0, 7)], 6),
        (g_row.at[pl.ds(0, 15)], 7), (f_got, 8), (c_own.at[1], 18), (count_got, 19), (count_all.at[pl.ds(0, 7)], 20),
    ):
        wait_for(buffer, send_sem, sem)

    @pl.when(jnp.logical_not(on_diagonal))
    def _():
        wait_for(c_turn.at[0], send_sem, 9)


def hand_over(doc_in, fis_in, doc_out, fis_out):
    doc_out[...] = doc_in[...]
    fis_out[...] = fis_in[...]


def per_device(acts, grads, pin, pout, seg, counts):
    tok, hidden = acts.shape
    width, span = grads.shape[1], tok // PARTS
    vmem, hbm, smem = (pl.BlockSpec(memory_space=m) for m in (pltpu.VMEM, pltpu.HBM, pltpu.SMEM))
    shapes = (jax.ShapeDtypeStruct((DOCS, COLS), BF16), jax.ShapeDtypeStruct((128, COLS), F32))
    results = pl.pallas_call(
        kernel,
        out_shape=(pltpu.VMEM((DOCS, COLS), BF16), pltpu.VMEM((128, COLS), F32)),
        in_specs=[hbm, hbm, hbm, hbm, hbm, smem],
        out_specs=(vmem, vmem),
        scratch_shapes=[
            pltpu.VMEM((tok, hidden), BF16),
            pltpu.VMEM((tok, width), BF16),
            pltpu.VMEM((RANK, hidden), BF16),
            pltpu.VMEM((RANK, width), BF16),
            pltpu.VMEM((DOCS, tok), jnp.int32),
            pltpu.VMEM((PARTS, RANK, span), F32),
            pltpu.VMEM((PARTS, RANK, span), F32),
            pltpu.VMEM((PARTS, RANK, span), BF16),
            pltpu.VMEM((PARTS, 3, QUART, span), F32),
            pltpu.VMEM((PARTS, 3, QUART, span), BF16),
            pltpu.VMEM((PARTS, QUART, span), BF16),
            pltpu.VMEM((PARTS, QUART, span), F32),
            pltpu.VMEM((PARTS, 3, QUART, span), BF16),
            pltpu.VMEM((PARTS, 3, QUART, span), F32),
            pltpu.VMEM((PARTS, QUART, span), F32),
            pltpu.VMEM((DOCS, tok), F32),
            pltpu.VMEM((QUART * DOCS, span), BF16),
            pltpu.VMEM((4, QUART, 128), BF16),
            pltpu.VMEM((2, 4, QUART, 128), BF16),
            pltpu.VMEM((4, QUART, 128), BF16),
            pltpu.VMEM((8, 2, DOCS, COLS), BF16),
            pltpu.VMEM((16, DOCS, COLS), BF16),
            pltpu.VMEM((136, COLS), F32),
            pltpu.VMEM((136, COLS), F32),
            pltpu.VMEM((8, 128), F32),
            pltpu.VMEM((8, 128), F32),
            pltpu.VMEM((8, 8, 128), F32),
            pltpu.SemaphoreType.DMA((3 + PARTS + CHUNKS,)),
            pltpu.SemaphoreType.DMA((40,)),
            pltpu.SemaphoreType.DMA((40,)),
        ],
        compiler_params=pltpu.CompilerParams(
            collective_id=0, has_side_effects=True, vmem_limit_bytes=60 * 1024 * 1024
        ),
        cost_estimate=pl.CostEstimate(flops=10**9, bytes_accessed=6 * 10**6, transcendentals=0),
        name="logra",
    )(acts, grads, pin.T, pout.T, seg, counts)
    return pl.pallas_call(
        hand_over,
        out_shape=shapes,
        in_specs=[vmem, vmem],
        out_specs=(vmem, vmem),
        compiler_params=pltpu.CompilerParams(vmem_limit_bytes=4 * 1024 * 1024),
        name="hand_over",
    )(*results)


def solution(mesh):
    return jax.shard_map(
        per_device,
        mesh=mesh,
        in_specs=(
            P("dp", "tensor"),
            P("dp", "tensor"),
            P("tensor", None),
            P("tensor", None),
            P(None, "dp"),
            P("dp"),
        ),
        out_specs=(P("dp", "tensor"), P("dp", "tensor")),
        check_vma=False,
    )
```

```python
import jax
import jax.numpy as jnp
from jax import lax
from jax.experimental import pallas as pl
from jax.experimental.pallas import tpu as pltpu
from jax.sharding import PartitionSpec as P

MESH = pl.DeviceIdType.MESH
F32 = jnp.float32
BF16 = jnp.bfloat16
RANK = 64
QUART = 16
CHUNKS = 4
PARTS = 4
DOCS = 32
COLS = 256
NT = (((1,), (1,)), ((), ()))
TN = (((0,), (0,)), ((), ()))


def dot(left, right, dims):
    return lax.dot_general(left, right, dims, preferred_element_type=F32)


def to_doc_rows(tile):
    turned = tile.astype(F32).T
    return jnp.concatenate([turned[DOCS * a : DOCS * (a + 1)] for a in range(4)], axis=1).astype(BF16)


def kernel(
    acts, grads, pin, pout, seg, counts, doc_out, fis_out,
    acts_v, grads_v, pin_v, pout_v, seg_v, dy_part, x_part, x_send, dy_got, x_got, dy_send2, x_send2, dy_got2, x_got2, dy_all,
    live_v, wide, sums, c_own, c_turn, g_col, g_row, f_send, f_got, count_own, count_got, count_all,
    in_sem, send_sem, recv_sem,
):
    i, j = lax.axis_index("dp"), lax.axis_index("tensor")
    k, c = i // 2, i % 2
    jx, jy = j // 4, j % 4
    x_peers = [(i, (jx + d) % 4 * 4 + jy) for d in (1, 2, 3)]
    y_peers = [(i, jx * 4 + (jy + d) % 4) for d in (1, 2, 3)]
    xy_peers = [(i, (jx + d) % 4 * 4 + (jy + e) % 4) for d in (2, 1, 3, 0) for e in (2, 1, 3, 0) if d or e]
    y_hi, z = k // 8, k % 8
    partner = ((k + 8) % 16) * 2 + c
    across = [(partner, jx * 4 + (jy + d) % 4) for d in range(4)]
    z_peers = [((y_hi * 8 + (z + d) % 8) * 2 + c, j) for d in (4, 3, 5, 2, 6, 1, 7)]
    sibling = (2 * k + 1 - c, j)
    turn_to = [((jx * 4 + (jy + d) % 4) * 2 + c, k) for d in range(4)]
    turn_from = [(j * 2 + c, k // 4 * 4 + (k + d) % 4) for d in range(4)]
    on_diagonal = j == k

    rows = acts.shape[0] // CHUNKS
    span = acts.shape[0] // PARTS

    def load(src, dst, n):
        copy = pltpu.make_async_copy(src, dst, in_sem.at[n])
        copy.start()
        return copy

    pin_load, pout_load = load(pin, pin_v, 1), load(pout, pout_v, 0)
    grads_load, acts_load = [], []

    def load_part(h):
        for n in range(h * CHUNKS // PARTS, (h + 1) * CHUNKS // PARTS):
            part = pl.ds(n * rows, rows)
            acts_load.append(load(acts.at[part], acts_v.at[part], 3 + PARTS + n))
        part = pl.ds(h * span, span)
        grads_load.append(load(grads.at[part], grads_v.at[part], 3 + h))

    load_part(0)

    barrier = pltpu.get_barrier_semaphore()

    def greet(peer):
        pl.semaphore_signal(barrier, inc=1, device_id=peer, device_id_type=MESH)

    for peer in xy_peers + z_peers + across + [sibling] + turn_to[1:] + turn_from[1:]:
        greet(peer)

    @pl.when(jnp.logical_not(on_diagonal))
    def _():
        greet(turn_to[0])
        greet(turn_from[0])

    for h in range(1, PARTS):
        load_part(h)
    seg_load = load(seg, seg_v, 2)

    def remote(src, dst, sem, peer):
        return pltpu.make_async_remote_copy(
            src_ref=src, dst_ref=dst, send_sem=send_sem.at[sem], recv_sem=recv_sem.at[sem],
            device_id=peer, device_id_type=MESH,
        )

    def wait_for(buffer, sems, sem):
        pltpu.make_async_copy(buffer, buffer, sems.at[sem]).wait()

    def project(h):
        for n in range(CHUNKS // PARTS):
            part = pl.ds(n * rows, rows)
            acts_load[h * CHUNKS // PARTS + n].wait()
            product = dot(pin_v[...], acts_v[pl.ds(h * span + n * rows, rows), :], NT)
            x_part[h, :, part] = product
            x_send[h, :, part] = product.astype(BF16)
        grads_load[h].wait()
        for n in range(CHUNKS // PARTS):
            part = pl.ds(n * rows, rows)
            dy_part[h, :, part] = dot(pout_v[...], grads_v[pl.ds(h * span + n * rows, rows), :], NT)

    def block(index):
        return pl.ds(pl.multiple_of(index * QUART, QUART), QUART)

    def send_parts(h):
        for d, peer in ((1, y_peers[1]), (2, y_peers[2]), (0, y_peers[0])):
            remote(x_send.at[h, block((jy + d + 1) % 4)], x_got.at[h, d], 22 + h, peer).start()
        for d, peer in ((1, x_peers[1]), (0, x_peers[0]), (2, x_peers[2])):
            remote(dy_part.at[h, block((jx + d + 1) % 4)], dy_got.at[h, d], 26 + h, peer).start()

    pout_load.wait()
    pin_load.wait()
    project(0)
    pl.semaphore_wait(barrier, jnp.where(on_diagonal, 33, 35))
    send_parts(0)
    for h in range(1, PARTS):
        project(h)
        send_parts(h)

    seg_load.wait()
    live = jnp.where(lax.broadcasted_iota(jnp.int32, seg.shape, 0) < counts[0], seg_v[...], 0).astype(F32)
    live_v[...] = live
    count_own[...] = jnp.full(count_own.shape, jnp.sum(live), F32)
    remote(count_own, count_got, 19, across[0]).start()

    for h in range(PARTS):
        wait_for(dy_got.at[h], recv_sem, 26 + h)
        dy_sum = dy_part[h, block(jx), :] + dy_got[h, 0] + dy_got[h, 1] + dy_got[h, 2]
        dy_all[h] = dy_sum
        dy_send2[h] = dy_sum.astype(BF16)
        for d, peer in ((1, y_peers[1]), (2, y_peers[2]), (0, y_peers[0])):
            remote(dy_send2.at[h], dy_got2.at[h, d], 30 + h, peer).start()
        wait_for(x_got.at[h], recv_sem, 22 + h)
        got = [x_got[h, d].astype(F32) for d in range(3)]
        x_send2[h] = x_part[h, block(jy), :] + got[0] + got[1] + got[2]
        for d, peer in ((1, x_peers[1]), (0, x_peers[0]), (2, x_peers[2])):
            remote(x_send2.at[h], x_got2.at[h, d], 34 + h, peer).start()

    wait_for(count_got, recv_sem, 19)
    count_all[z] = count_own[...] + count_got[...]
    for peer in z_peers:
        remote(count_all.at[z], count_all.at[z], 20, peer).start()

    both = jnp.zeros((2 * QUART, QUART * DOCS), F32)
    for h in range(PARTS):
        wait_for(dy_got2.at[h], recv_sem, 30 + h)
        got = [dy_got2[h, d].astype(F32) for d in range(3)]
        dy_full = dy_all[h] + got[0] + got[1] + got[2]
        mask = live_v[:, h * span : (h + 1) * span]
        for a in range(QUART):
            wide[a * DOCS : (a + 1) * DOCS, :] = (mask * dy_full[a : a + 1, :]).astype(BF16)
        wait_for(x_got2.at[h], recv_sem, 34 + h)
        x_full = x_send2[h] + x_got2[h, 0] + x_got2[h, 1] + x_got2[h, 2]
        x_high = x_full.astype(BF16)
        x_low = (x_full - x_high.astype(F32)).astype(BF16)
        both = both + dot(jnp.concatenate([x_high, x_low], axis=0), wide[...], NT)
    total = (both[:QUART] + both[QUART:]).astype(BF16)
    for q in range(4):
        sums[q] = total[:, q * 128 : (q + 1) * 128]

    for d in (1, 2, 3):
        remote(sums.at[(jy + d) % 4], c_turn.at[jy], 5, turn_to[d]).start()

    @pl.when(jnp.logical_not(on_diagonal))
    def _():
        remote(sums.at[jy], c_turn.at[jy], 9, turn_to[0]).start()

    for d, peer in enumerate(across):
        remote(sums.at[(jy + d) % 4], c_own.at[1, jy], 18, peer).start()
    for d, peer in enumerate(y_peers):
        remote(sums.at[(jy + d + 1) % 4], c_own.at[0, jy], 4, peer).start()
    c_own[0, jy] = sums[jy]

    @pl.when(on_diagonal)
    def _():
        c_turn[jy] = sums[jy]

    wait_for(c_own.at[0, pl.ds(0, 3)], recv_sem, 4)
    own = to_doc_rows(c_own[0].reshape(RANK, 128))
    doc_out[...] = own
    g_col[z, y_hi] = own
    wait_for(c_own.at[1], recv_sem, 18)
    g_col[z, 1 - y_hi] = to_doc_rows(c_own[1].reshape(RANK, 128))
    for peer in z_peers:
        remote(g_col.at[z], g_col.at[z], 6, peer).start()

    wait_for(c_turn.at[pl.ds(0, 3)], recv_sem, 5)

    @pl.when(jnp.logical_not(on_diagonal))
    def _():
        wait_for(c_turn.at[0], recv_sem, 9)

    slot = j % 8 * 2 + j // 8
    g_row[slot] = to_doc_rows(c_turn[...].reshape(RANK, 128))
    for peer in xy_peers:
        remote(g_row.at[slot], g_row.at[slot], 7, peer).start()

    wait_for(count_all.at[pl.ds(0, 7)], recv_sem, 20)
    live_tokens = jnp.sum(count_all[:, 0, 0:1])
    wait_for(g_col.at[pl.ds(0, 7)], recv_sem, 6)
    columns = g_col[...].reshape(16 * DOCS, COLS)
    wait_for(g_row.at[pl.ds(0, 15)], recv_sem, 7)

    def fisher_rows(half):
        left = g_row[:, :, pl.ds(pl.multiple_of(half * 128, 128), 128)].reshape(16 * DOCS, 128)
        return dot(left, columns, TN)

    f_send[:128] = fisher_rows(1 - c)
    f_send[128:] = jnp.full((8, COLS), live_tokens, F32)
    remote(f_send, f_got, 8, sibling).start()
    mine = fisher_rows(c)
    wait_for(f_got, recv_sem, 8)
    fis_out[...] = (mine + f_got[:128]) / (f_got[128:129, :] + live_tokens)

    for h in range(PARTS):
        for buffer, sem in ((x_got, 22), (dy_got, 26), (dy_got2, 30), (x_got2, 34)):
            wait_for(buffer.at[h], send_sem, sem + h)
    for buffer, sem in (
        (c_own.at[0, pl.ds(0, 3)], 4), (c_turn.at[pl.ds(0, 3)], 5), (g_col.at[pl.ds(0, 7)], 6),
        (g_row.at[pl.ds(0, 15)], 7), (f_got, 8), (c_own.at[1], 18), (count_got, 19), (count_all.at[pl.ds(0, 7)], 20),
    ):
        wait_for(buffer, send_sem, sem)

    @pl.when(jnp.logical_not(on_diagonal))
    def _():
        wait_for(c_turn.at[0], send_sem, 9)


def hand_over(doc_in, fis_in, doc_out, fis_out):
    doc_out[...] = doc_in[...]
    fis_out[...] = fis_in[...]


def per_device(acts, grads, pin, pout, seg, counts):
    tok, hidden = acts.shape
    width, span = grads.shape[1], tok // PARTS
    vmem, hbm, smem = (pl.BlockSpec(memory_space=m) for m in (pltpu.VMEM, pltpu.HBM, pltpu.SMEM))
    shapes = (jax.ShapeDtypeStruct((DOCS, COLS), BF16), jax.ShapeDtypeStruct((128, COLS), F32))
    results = pl.pallas_call(
        kernel,
        out_shape=(pltpu.VMEM((DOCS, COLS), BF16), pltpu.VMEM((128, COLS), F32)),
        in_specs=[hbm, hbm, hbm, hbm, hbm, smem],
        out_specs=(vmem, vmem),
        scratch_shapes=[
            pltpu.VMEM((tok, hidden), BF16),
            pltpu.VMEM((tok, width), BF16),
            pltpu.VMEM((RANK, hidden), BF16),
            pltpu.VMEM((RANK, width), BF16),
            pltpu.VMEM((DOCS, tok), jnp.int32),
            pltpu.VMEM((PARTS, RANK, span), F32),
            pltpu.VMEM((PARTS, RANK, span), F32),
            pltpu.VMEM((PARTS, RANK, span), BF16),
            pltpu.VMEM((PARTS, 3, QUART, span), F32),
            pltpu.VMEM((PARTS, 3, QUART, span), BF16),
            pltpu.VMEM((PARTS, QUART, span), BF16),
            pltpu.VMEM((PARTS, QUART, span), F32),
            pltpu.VMEM((PARTS, 3, QUART, span), BF16),
            pltpu.VMEM((PARTS, 3, QUART, span), F32),
            pltpu.VMEM((PARTS, QUART, span), F32),
            pltpu.VMEM((DOCS, tok), F32),
            pltpu.VMEM((QUART * DOCS, span), BF16),
            pltpu.VMEM((4, QUART, 128), BF16),
            pltpu.VMEM((2, 4, QUART, 128), BF16),
            pltpu.VMEM((4, QUART, 128), BF16),
            pltpu.VMEM((8, 2, DOCS, COLS), BF16),
            pltpu.VMEM((16, DOCS, COLS), BF16),
            pltpu.VMEM((136, COLS), F32),
            pltpu.VMEM((136, COLS), F32),
            pltpu.VMEM((8, 128), F32),
            pltpu.VMEM((8, 128), F32),
            pltpu.VMEM((8, 8, 128), F32),
            pltpu.SemaphoreType.DMA((3 + PARTS + CHUNKS,)),
            pltpu.SemaphoreType.DMA((40,)),
            pltpu.SemaphoreType.DMA((40,)),
        ],
        compiler_params=pltpu.CompilerParams(
            collective_id=0, has_side_effects=True, vmem_limit_bytes=60 * 1024 * 1024
        ),
        cost_estimate=pl.CostEstimate(flops=10**9, bytes_accessed=6 * 10**6, transcendentals=0),
        name="logra",
    )(acts, grads, pin.T, pout.T, seg, counts)
    return pl.pallas_call(
        hand_over,
        out_shape=shapes,
        in_specs=[vmem, vmem],
        out_specs=(vmem, vmem),
        compiler_params=pltpu.CompilerParams(vmem_limit_bytes=4 * 1024 * 1024),
        name="hand_over",
    )(*results)


def solution(mesh):
    return jax.shard_map(
        per_device,
        mesh=mesh,
        in_specs=(
            P("dp", "tensor"),
            P("dp", "tensor"),
            P("tensor", None),
            P("tensor", None),
            P(None, "dp"),
            P("dp"),
        ),
        out_specs=(P("dp", "tensor"), P("dp", "tensor")),
        check_vma=False,
    )
```
